256 devices in a mesh: row: 16 (over y, x), col: 16 (over z, core).
Axes of the slice: x: 4, y: 4, z: 8, core: 2. Of those that a mesh axis runs over, the one named last changes fastest.
Arguments:
- front: float32 [8, 16, 128, 8, 16, 128], P(None, 'row', None, None, 'col'), as said below
- block_slots: int32 [128], replicated, may hold values from 0 to 127, as said below
- rows_first: int32 [79], replicated, may hold values from 4 to 127, as said below
- rows_second: int32 [105], replicated, may hold values from 8 to 127, as said below
Outputs:
- factored: float32 [8, 16, 128, 8, 16, 128], P(None, 'row', None, None, 'col')
The draws below stay inside these ranges and needn't reach their ends.
Inputs may be any that keep to these rules, and one draw needn't show every extreme that they name: front is symmetric, and its square on the slots of blocks 0 to 7 is positive definite. `block_slots`: each slot appears once. `rows_second`: 105 distinct block numbers in increasing order; 8 and 127 are always among them. `rows_first`: 4, 5, 6, 7, then 79 - 4 distinct block numbers in increasing order, all of them in rows_second, 127 always among them.
All inputs are finite; a program needn't handle non-finite values.
Results may differ from the reference program's by a relative error of at most 0.00028.
Values sent between devices are 32-bit elements; how exact they have to be, the bound alone decides.
A program may use at most 128 MiB of HBM per device.

```python
import jax
import jax.numpy as jnp
from jax import lax

BS = 128
PB = 4
NB = 128
RB = 8
CB = 8
R2 = 105
R1 = 79


def block_order(key):
    return jax.random.permutation(jax.random.fold_in(key, 11), NB).astype(jnp.int32)


def row_lists(key):
    interior = jax.random.permutation(jax.random.fold_in(key, 23), NB - 10).astype(jnp.int32) + 9
    ends = jnp.array([8, NB - 1], dtype=jnp.int32)
    second_list = jnp.sort(jnp.concatenate([ends, interior[:R2 - 2]]))
    first_extra = jnp.sort(jnp.concatenate([ends[1:], interior[:R1 - 5]]))
    first_list = jnp.concatenate([jnp.arange(4, 8, dtype=jnp.int32), first_extra])
    return (first_list, second_list)


def draw_block_slots(key, part):
    return block_order(key)


def draw_rows_first(key, part):
    return row_lists(key)[0]


def draw_rows_second(key, part):
    return row_lists(key)[1]


def draw_front(key, part):
    matrix_order = NB * BS
    entries = jax.random.truncated_normal(jax.random.fold_in(key, 31), -4.0, 4.0, (matrix_order, matrix_order), jnp.float32)
    symmetric = (entries + entries.T) * 0.70710678
    order = block_order(key)
    block_ids = jnp.arange(NB, dtype=jnp.int32)
    first_mask = jnp.any(block_ids[:, None] == order[None, :PB], axis=1).astype(jnp.float32)
    second_mask = jnp.any(block_ids[:, None] == order[None, PB:2 * PB], axis=1).astype(jnp.float32)
    first_cells = jnp.repeat(first_mask, BS)
    second_cells = jnp.repeat(second_mask, BS)
    cross = first_cells[:, None] * second_cells[None, :]
    cross = cross + cross.T
    symmetric = symmetric * (1.0 - 0.85 * cross)
    same_panel = first_cells[:, None] * first_cells[None, :] + second_cells[:, None] * second_cells[None, :]
    symmetric = symmetric + 0.03 * same_panel
    diagonal_boost = jax.random.uniform(jax.random.fold_in(key, 37), (matrix_order,), jnp.float32, 56.0, 72.0)
    diagonal_boost = diagonal_boost * (first_cells + second_cells)
    positions = jnp.arange(matrix_order, dtype=jnp.int32)
    matrix = symmetric.at[positions, positions].add(diagonal_boost)
    return matrix.reshape(RB, NB // RB, BS, CB, NB // CB, BS)


def setup_inputs(seed: int = 0) -> dict:
    splits = jax.random.split(jax.random.key(seed), 5)
    return {
        "front": draw_front(jax.random.fold_in(splits[4], 71), 0),
        "block_slots": draw_block_slots(jax.random.fold_in(splits[4], 71), 0),
        "rows_first": draw_rows_first(jax.random.fold_in(splits[4], 71), 0),
        "rows_second": draw_rows_second(jax.random.fold_in(splits[4], 71), 0),
    }


def block_indices(slot_list):
    offsets = jnp.arange(BS, dtype=jnp.int32)
    return (slot_list.astype(jnp.int32)[:, None] * BS + offsets[None, :]).reshape(-1)

def reference(front, block_slots, rows_first, rows_second):
    matrix_order = NB * BS
    matrix = front.reshape(matrix_order, matrix_order)
    identity = jnp.eye(PB * BS, dtype=jnp.float32)
    for panel_index, row_list in ((0, rows_first), (1, rows_second)):
        col_index = block_indices(block_slots[PB * panel_index:PB * (panel_index + 1)])
        row_index = block_indices(block_slots[row_list])
        diag_block = matrix[col_index[:, None], col_index[None, :]]
        lower_factor = jnp.linalg.cholesky(diag_block)
        inverse = lax.linalg.triangular_solve(lower_factor, identity, left_side=True, lower=True)
        row_panel = matrix[row_index[:, None], col_index[None, :]]
        solved = jnp.dot(row_panel, inverse.T, precision=lax.Precision.HIGHEST)
        spread = jnp.zeros((matrix_order, PB * BS), dtype=jnp.float32).at[row_index].set(solved)
        matrix = matrix - jnp.dot(spread, spread.T, precision=lax.Precision.HIGHEST)
        matrix = matrix.at[row_index[:, None], col_index[None, :]].set(solved)
        matrix = matrix.at[col_index[:, None], col_index[None, :]].set(lower_factor)
    return matrix.reshape(front.shape)
```

```python
import functools

import jax
import jax.numpy as jnp
from jax import lax
from jax.experimental import pallas as pl
from jax.experimental.pallas import tpu as pltpu
from jax.sharding import PartitionSpec as P

BS = 128
NP = 8
GRID = 16
NX = 4
NZ = 8
RB = 8
HALF = RB * BS // 2
PAIRS = [(k, i) for k in range(NP) for i in range(k, NP)]
FIRST = [PAIRS.index((k, k)) for k in range(NP)]
DROWS = len(PAIRS) * BS
DCHUNK = DROWS // (2 * NZ)
MESH = pl.DeviceIdType.MESH
HIGHEST = lax.Precision.HIGHEST
SMEM = pl.BlockSpec(memory_space=pltpu.SMEM)
VMEM = pl.BlockSpec(memory_space=pltpu.VMEM)

T_POS, T_OWN, T_M1R, T_M2R, T_M1C, T_M2C, T_BNUM, T_KCOL, T_ROW, T_ROWN = range(0, 80, 8)


def table_kernel(slots_ref, first_ref, second_ref, tab_ref):
    own_row = lax.axis_index("row")
    own_col = lax.axis_index("col")
    for index in range(8):
        for base in (T_M1R, T_M2R, T_M1C, T_M2C):
            tab_ref[base + index] = 0
        tab_ref[T_BNUM + index] = NP
        tab_ref[T_KCOL + index] = NP
    for k in range(NP):
        slot = slots_ref[k]
        high, low = slot // GRID, slot % GRID
        tab_ref[T_POS + k] = high
        tab_ref[T_ROW + k] = high
        tab_ref[T_OWN + k] = (low == own_col).astype(jnp.int32)
        tab_ref[T_ROWN + k] = (low == own_row).astype(jnp.int32)

        @pl.when(low == own_col)
        def _():
            tab_ref[T_KCOL + high] = k

        @pl.when(low == own_row)
        def _():
            tab_ref[T_BNUM + high] = k

    for list_ref, base_row, base_col in ((first_ref, T_M1R, T_M1C), (second_ref, T_M2R, T_M2C)):

        def mark(entry, carry, list_ref=list_ref, base_row=base_row, base_col=base_col):
            slot = slots_ref[list_ref[entry]]
            high, low = slot // GRID, slot % GRID

            @pl.when(low == own_row)
            def _():
                tab_ref[base_row + high] = 1

            @pl.when(low == own_col)
            def _():
                tab_ref[base_col + high] = 1

            return carry

        lax.fori_loop(0, list_ref.shape[0], mark, 0)


def make_table(slots, first, second):
    return pl.pallas_call(
        table_kernel,
        out_shape=jax.ShapeDtypeStruct((80,), jnp.int32),
        in_specs=[SMEM] * 3,
        out_specs=SMEM,
        name="table",
    )(slots, first, second)


class Links:
    def __init__(self, send, recv):
        self.send, self.recv, self.used = send, recv, 0

    def copy(self, src, dst, row, col):
        op = pltpu.make_async_remote_copy(
            src_ref=src,
            dst_ref=dst,
            send_sem=self.send.at[self.used],
            recv_sem=self.recv.at[self.used],
            device_id=(row, col),
            device_id_type=MESH,
        )
        self.used += 1
        op.start()
        return op


def wait_all(ops):
    for op in ops:
        op.wait()


def comm_kernel(tab_ref, front_ref, d_ref, vp_ref, vq_ref, dc, vc, dr, vr, drz, vrz, dx, send, recv, local):
    p = lax.axis_index("row")
    q = lax.axis_index("col")
    x, y = p % NX, p // NX
    z, h = q // 2, q % 2
    other = 1 - h
    links = Links(send, recv)
    sibling = (p, q + 1 - 2 * h)
    zright = (p, (q + 2) % GRID)
    zleft = (p, (q + GRID - 2) % GRID)

    def at_x(d):
        return (y * NX + (x + d + NX) % NX, q)

    def at_y(d):
        return (((y + d + NX) % NX) * NX + x, q)

    partners = [sibling, zright, zleft] + [at_x(d) for d in (1, 2, 3)] + [at_y(d) for d in (1, 2, 3)]
    barrier = pltpu.get_barrier_semaphore()
    for row, col in partners:
        pl.semaphore_signal(barrier, inc=1, device_id=(row, col), device_id_type=MESH)

    @pl.when(p != q)
    def _():
        pl.semaphore_signal(barrier, inc=1, device_id=(q, p), device_id_type=MESH)

    for index, (k, i) in enumerate(PAIRS):
        start = tab_ref[T_ROW + i] * (BS * RB) + tab_ref[T_POS + k]
        mine = tab_ref[T_OWN + k] * tab_ref[T_ROWN + i]
        block = front_ref[pl.ds(start, BS, RB), :]
        dc[pl.ds(index * BS, BS), :] = jnp.where(mine > 0, block, 0.0)
    for k in range(NP):
        start = tab_ref[T_POS + k]
        mine = tab_ref[T_OWN + k]

        def pack(a, carry, k=k, start=start, mine=mine):
            block = front_ref[pl.ds(start + a * (BS * RB), BS, RB), :]
            vc[pl.ds(pl.multiple_of(k * RB * BS + a * BS, BS), BS), :] = jnp.where(mine > 0, block, 0.0)
            return carry

        lax.fori_loop(0, RB, pack, 0)

    pl.semaphore_wait(barrier, len(partners) + (p != q).astype(jnp.int32))

    def chunk(ref, rows, zz, hh, lo=0, size=None):
        size = rows if size is None else size
        return ref.at[pl.ds(pl.multiple_of((zz * 2 + hh) * rows + lo, 8), size), :]

    def reduce_to_z(buf, rows, pair_buf, ring_buf):
        ops = []
        for zz in range(NZ):
            ops.append(links.copy(chunk(buf, rows, zz, other), pair_buf.at[pl.ds(zz * rows, rows), :], *sibling))
        wait_all(ops)

        def add_pair(zz, carry):
            target = chunk(buf, rows, zz, h)
            target[...] += pair_buf[pl.ds(pl.multiple_of(zz * rows, 8), rows), :]
            return carry

        lax.fori_loop(0, NZ, add_pair, 0)
        split = rows // 2
        for step in range(1, 5):
            far = 5 - step
            if step == 1:
                right = chunk(buf, rows, (z + 4) % NZ, h, 0, split)
                left = chunk(buf, rows, (z + 4) % NZ, h, split, split)
                to_right = ring_buf.at[0, step - 1, pl.ds(0, split), :]
                to_left = ring_buf.at[1, step - 1, pl.ds(split, split), :]
            else:
                right = chunk(buf, rows, (z + far) % NZ, h)
                left = chunk(buf, rows, (z + NZ - far) % NZ, h)
                to_right = ring_buf.at[0, step - 1]
                to_left = ring_buf.at[1, step - 1]
            wait_all([links.copy(right, to_right, *zright), links.copy(left, to_left, *zleft)])
            for side, dest in ((0, (z + far - 1) % NZ), (1, (z + NZ - far + 1) % NZ)):
                lo, size = (0, rows) if step > 1 else (side * split, split)
                target = chunk(buf, rows, dest, h, lo, size)
                target[...] += ring_buf[side, step - 1, pl.ds(lo, size), :]

    def gather_z(buf, rows):
        pair = [links.copy(chunk(buf, rows, z, h), chunk(buf, rows, z, h), *sibling)]
        split = rows // 2
        for step in range(1, 5):
            ahead = (z + NZ - step + 1) % NZ
            behind = (z + step - 1) % NZ
            if step < 4:
                right = chunk(buf, rows, ahead, h)
                left = chunk(buf, rows, behind, h)
            else:
                right = chunk(buf, rows, ahead, h, 0, split)
                left = chunk(buf, rows, behind, h, split, split)
            wait_all([links.copy(right, right, *zright), links.copy(left, left, *zleft)])
            got = [(z + NZ - step) % NZ, (z + step) % NZ][: 2 if step < 4 else 1]
            for zz in got:
                pair.append(links.copy(chunk(buf, rows, zz, h), chunk(buf, rows, zz, h), *sibling))
        wait_all(pair)

    reduce_to_z(dc, DCHUNK, dr, drz)
    quarter = DCHUNK // 4
    mine = chunk(dc, DCHUNK, z, h)
    base = (z * 2 + h) * DCHUNK

    def part(ref, xx):
        return ref.at[pl.ds(pl.multiple_of(base + xx * quarter, 8), quarter), :]

    wait_all([links.copy(part(dc, (x + d) % NX), dx.at[0, d - 1], *at_x(d)) for d in (1, 2, 3)])
    own = part(dc, x)
    own[...] += dx[0, 0] + dx[0, 1] + dx[0, 2]
    wait_all([links.copy(own, dx.at[1, d - 1], *at_y(d)) for d in (1, 2, 3)])
    part(d_ref, x)[...] = own[...] + (dx[1, 0] + dx[1, 1] + dx[1, 2])
    wait_all([links.copy(part(d_ref, x), part(d_ref, x), *at_x(d)) for d in (1, 2, 3)])
    gather_z(d_ref, DCHUNK)

    reduce_to_z(vc, HALF, vr, vrz)
    chunk(vp_ref, HALF, z, h)[...] = chunk(vc, HALF, z, h)[...]
    index = links.used
    links.used += 1

    @pl.when(p != q)
    def _():
        op = pltpu.make_async_remote_copy(
            src_ref=chunk(vp_ref, HALF, z, h),
            dst_ref=chunk(vq_ref, HALF, z, h),
            send_sem=send.at[index],
            recv_sem=recv.at[index],
            device_id=(q, p),
            device_id_type=MESH,
        )
        op.start()
        op.wait_send()
        back = pltpu.make_async_remote_copy(
            src_ref=chunk(vp_ref, HALF, z, h),
            dst_ref=chunk(vq_ref, HALF, p // 2, p % 2),
            send_sem=send.at[index],
            recv_sem=recv.at[index],
            device_id=(q, p),
            device_id_type=MESH,
        )
        back.wait_recv()

    @pl.when(p == q)
    def _():
        op = pltpu.make_async_copy(chunk(vp_ref, HALF, z, h), chunk(vq_ref, HALF, z, h), local.at[0])
        op.start()
        op.wait()

    gather_z(vp_ref, HALF)

    lo, hi = HALF // 2, HALF // 4

    def along(axis, xx, yy, begin, size):
        return chunk(vq_ref, HALF, yy * 2 + xx // 2, xx % 2, begin, size)

    def neighbours(axis):
        return (at_x(1), at_x(-1)) if axis == "x" else (at_y(1), at_y(-1))

    for first_pass in (True, False):
        for step in (1, 2):
            ops = []
            for begin, axis in ((0, "x"), (lo, "y")) if first_pass else ((0, "y"), (lo, "x")):
                plus, minus = neighbours(axis)
                for side, target in ((0, plus), (1, minus)):
                    shift = 0 if step == 1 else (NX - 1 if side == 0 else 1)
                    start, size = (begin, lo) if step == 1 else (begin + side * hi, hi)
                    for line in range(1 if first_pass else NX):
                        if axis == "x":
                            xx = (x + shift) % NX
                            yy = y if first_pass else line
                        else:
                            yy = (y + shift) % NX
                            xx = x if first_pass else line
                        ref = along(axis, xx, yy, start, size)
                        ops.append(links.copy(ref, ref, *target))
            wait_all(ops)


def exchange(table, front):
    copies = 128
    return pl.pallas_call(
        comm_kernel,
        out_shape=[
            jax.ShapeDtypeStruct((DROWS, BS), jnp.float32),
            jax.ShapeDtypeStruct((GRID * HALF, BS), jnp.float32),
            jax.ShapeDtypeStruct((GRID * HALF, BS), jnp.float32),
        ],
        in_specs=[SMEM, VMEM],
        out_specs=[VMEM] * 3,
        scratch_shapes=[
            pltpu.VMEM((DROWS, BS), jnp.float32),
            pltpu.VMEM((GRID * HALF, BS), jnp.float32),
            pltpu.VMEM((DROWS // 2, BS), jnp.float32),
            pltpu.VMEM((GRID * HALF // 2, BS), jnp.float32),
            pltpu.VMEM((2, 4, DCHUNK, BS), jnp.float32),
            pltpu.VMEM((2, 4, HALF, BS), jnp.float32),
            pltpu.VMEM((2, 3, DCHUNK // 4, BS), jnp.float32),
            pltpu.SemaphoreType.DMA((copies,)),
            pltpu.SemaphoreType.DMA((copies,)),
            pltpu.SemaphoreType.DMA((1,)),
        ],
        compiler_params=pltpu.CompilerParams(
            collective_id=0, has_side_effects=True, vmem_limit_bytes=56 * 2**20
        ),
        name="exchange",
    )(table, front)


def row_of(value, index):
    return jnp.broadcast_to(value[index : index + 1, :], value.shape)


def eliminate(rows, extra, step):
    sub = lax.broadcasted_iota(jnp.int32, (8, BS), 0)
    cols = [jnp.broadcast_to(rows[:, 8 * step + c : 8 * step + c + 1], (8, BS)) for c in range(8)]
    pivots = jnp.zeros((8, BS), jnp.float32)
    for c in range(8):
        pivot = row_of(cols[c], c)
        mult = jnp.where(sub > c, cols[c] * (1.0 / pivot), 0.0)
        pivots = jnp.where(sub == c, pivot, pivots)
        for later in range(c + 1, 8):
            cols[later] = cols[later] - mult * row_of(cols[later], c)
        rows = rows - mult * row_of(rows, c)
        extra = extra - mult * row_of(extra, c)
    scale = lax.rsqrt(pivots)
    return rows * scale, extra * scale


def factor_block(block):
    row = lax.broadcasted_iota(jnp.int32, (BS, BS), 0)
    col = lax.broadcasted_iota(jnp.int32, (BS, BS), 1)
    lane = lax.broadcasted_iota(jnp.int32, (8, BS), 1)
    work = jnp.concatenate([block, (row == col).astype(jnp.float32)], axis=1)
    upper, inverse = [], []
    for step in range(BS // 8):
        rows, extra = eliminate(work[:8, :BS], work[:8, BS:], step)
        rows = jnp.where(lane >= 8 * step, rows, 0.0)
        upper.append(rows)
        inverse.append(extra)
        if step < BS // 8 - 1:
            work = work[8:]
            both = jnp.concatenate([rows, extra], axis=1)
            turned = rows.T[8 * step + 8 :]
            for c in range(8):
                work = work - jnp.broadcast_to(turned[:, c : c + 1], work.shape) * jnp.broadcast_to(
                    both[c : c + 1, :], work.shape
                )
    upper = jnp.concatenate(upper, axis=0)
    return jnp.where(col >= row, upper, 0.0), jnp.concatenate(inverse, axis=0)


def dot_nt(a, b, precision=HIGHEST):
    return lax.dot_general(a, b, (((1,), (1,)), ((), ())), precision=precision, preferred_element_type=jnp.float32)


def factor_kernel(d_ref, l_ref, inv_ref, work):
    work[...] = d_ref[...]
    for k in range(NP):
        top = FIRST[k] * BS
        upper, inverse = factor_block(work[pl.ds(top, BS), :])
        l_ref[pl.ds(top, BS), :] = upper.T
        inv_ref[k] = inverse
        if k == NP - 1:
            break
        below = dot_nt(work[pl.ds(top + BS, (NP - 1 - k) * BS), :], inverse)
        l_ref[pl.ds(top + BS, (NP - 1 - k) * BS), :] = below
        for j in range(k + 1, NP):
            part = below[(j - k - 1) * BS :]
            rows = pl.ds(FIRST[j] * BS, (NP - j) * BS)
            work[rows, :] -= dot_nt(part, part[:BS])


def factor(d):
    return pl.pallas_call(
        factor_kernel,
        out_shape=[
            jax.ShapeDtypeStruct((DROWS, BS), jnp.float32),
            jax.ShapeDtypeStruct((NP, BS, BS), jnp.float32),
        ],
        in_specs=[VMEM],
        out_specs=[VMEM] * 2,
        scratch_shapes=[pltpu.VMEM((DROWS, BS), jnp.float32)],
        compiler_params=pltpu.CompilerParams(vmem_limit_bytes=56 * 2**20),
        name="factor",
    )(d)


def split(value):
    high = value.astype(jnp.bfloat16)
    return high, (value - high.astype(jnp.float32)).astype(jnp.bfloat16)


def dot3(a, b):
    (ah, al), (bh, bl) = a, b
    dims = (((1,), (1,)), ((), ()))
    mm = functools.partial(lax.dot_general, dimension_numbers=dims, preferred_element_type=jnp.float32)
    return mm(ah, bh) + (mm(ah, bl) + mm(al, bh))


WIDE = 2 * BS
TILE = 256


def update_kernel(tab_ref, front_ref, vp_ref, vq_ref, l_ref, inv_ref, out_ref, sh, sl, sf, lh, ll, ih, il):
    def block(i, k):
        return l_ref[pl.ds((FIRST[k] + i - k) * BS, BS), :]

    zero = jnp.zeros((BS, BS), jnp.float32)
    for wide in range(NP // 2):
        a, b = 2 * wide, 2 * wide + 1
        cross = -lax.dot_general(
            inv_ref[b],
            lax.dot_general(block(b, a), inv_ref[a], (((1,), (0,)), ((), ())), precision=HIGHEST),
            (((1,), (0,)), ((), ())),
            precision=HIGHEST,
        )
        inverse = jnp.concatenate(
            [jnp.concatenate([inv_ref[a], zero], axis=1), jnp.concatenate([cross, inv_ref[b]], axis=1)], axis=0
        )
        ih[wide], il[wide] = split(inverse)
        for before in range(wide):
            c, d = 2 * before, 2 * before + 1
            piece = jnp.concatenate(
                [
                    jnp.concatenate([block(a, c), block(a, d)], axis=1),
                    jnp.concatenate([block(b, c), block(b, d)], axis=1),
                ],
                axis=0,
            )
            rows, cols = pl.ds(wide * WIDE, WIDE), pl.ds(before * WIDE, WIDE)
            lh[rows, cols], ll[rows, cols] = split(piece)

    for part, (v_ref, first, second) in enumerate(((vp_ref, T_M1R, T_M2R), (vq_ref, T_M1C, T_M2C))):

        def solve(t, carry, part=part, v_ref=v_ref, first=first, second=second):
            low = t * TILE
            rows = pl.ds(pl.multiple_of(part * RB * BS + low, TILE), TILE)
            which = lax.broadcasted_iota(jnp.int32, (TILE, WIDE), 0) // BS
            keep = []
            for base in (first, second):
                even, odd = tab_ref[base + 2 * t], tab_ref[base + 2 * t + 1]
                keep.append(jnp.where(which == 0, even, odd) > 0)
            for wide in range(NP // 2):
                raw = jnp.concatenate(
                    [
                        v_ref[pl.ds(pl.multiple_of(k * RB * BS + low, TILE), TILE), :]
                        for k in (2 * wide, 2 * wide + 1)
                    ],
                    axis=1,
                )
                if wide:
                    old = pl.ds(0, wide * WIDE)
                    down = pl.ds(wide * WIDE, WIDE)
                    raw = raw - dot3((sh[rows, old], sl[rows, old]), (lh[down, old], ll[down, old]))
                solved = dot3(split(raw), (ih[wide], il[wide]))
                solved = jnp.where(keep[wide // 2], solved, 0.0)
                cols = pl.ds(wide * WIDE, WIDE)
                sh[rows, cols], sl[rows, cols] = split(solved)
                if part == 0:
                    for k in (2 * wide, 2 * wide + 1):
                        sf[k, pl.ds(pl.multiple_of(low, TILE), TILE), :] = solved[:, (k % 2) * BS : (k % 2 + 1) * BS]
            return carry

        lax.fori_loop(0, RB * BS // TILE, solve, 0)

    for t in range(RB * BS // TILE):
        rows = pl.ds(t * TILE, TILE)

        def update(u, carry, t=t, rows=rows):
            cols = pl.ds(pl.multiple_of(RB * BS + u * WIDE, WIDE), WIDE)
            term = dot3((sh[rows, :], sl[rows, :]), (sh[cols, :], sl[cols, :]))
            for a in range(2):
                for b in range(2):
                    row_block, col_block = 2 * t + a, 2 * u + b
                    place = pl.ds(row_block * BS * RB + col_block, BS, RB)
                    out_ref[place, :] = front_ref[place, :] - term[a * BS : (a + 1) * BS, b * BS : (b + 1) * BS]
            return carry

        lax.fori_loop(0, RB // 2, update, 0)

    for k in range(NP):
        base = T_M1R if k < NP // 2 else T_M2R

        @pl.when(tab_ref[T_OWN + k] > 0)
        def _():
            for a in range(RB):
                place = pl.ds(a * BS * RB + tab_ref[T_POS + k], BS, RB)
                number = tab_ref[T_BNUM + a]

                @pl.when((number >= NP) & (tab_ref[base + a] > 0))
                def _():
                    out_ref[place, :] = sf[k, pl.ds(a * BS, BS), :]

                @pl.when((number < NP) & ((number >= NP // 2) | (k < NP // 2)))
                def _():
                    start = (FIRST[k] + jnp.maximum(number - k, 0)) * BS
                    piece = l_ref[pl.ds(pl.multiple_of(start, BS), BS), :]
                    out_ref[place, :] = jnp.where(number >= k, piece, 0.0)


def update(table, front, vp, vq, lower, inverses):
    order = NP * BS
    return pl.pallas_call(
        update_kernel,
        out_shape=jax.ShapeDtypeStruct(front.shape, jnp.float32),
        in_specs=[SMEM] + [VMEM] * 5,
        out_specs=VMEM,
        scratch_shapes=[
            pltpu.VMEM((2 * RB * BS, order), jnp.bfloat16),
            pltpu.VMEM((2 * RB * BS, order), jnp.bfloat16),
            pltpu.VMEM((NP, RB * BS, BS), jnp.float32),
            pltpu.VMEM((order, order), jnp.bfloat16),
            pltpu.VMEM((order, order), jnp.bfloat16),
            pltpu.VMEM((NP // 2, WIDE, WIDE), jnp.bfloat16),
            pltpu.VMEM((NP // 2, WIDE, WIDE), jnp.bfloat16),
        ],
        compiler_params=pltpu.CompilerParams(vmem_limit_bytes=60 * 2**20),
        name="update",
    )(table, front, vp, vq, lower, inverses)


def on_device(front, block_slots, rows_first, rows_second):
    table = make_table(block_slots, rows_first, rows_second)
    flat = front.reshape(RB * BS * RB, BS)
    d, vp, vq = exchange(table, flat)
    lower, inverses = factor(d)
    return update(table, flat, vp, vq, lower, inverses).reshape(front.shape)


def solution(mesh):
    placed = (P(None, "row", None, None, "col", None), P(), P(), P())
    return jax.shard_map(
        on_device,
        mesh=mesh,
        in_specs=placed,
        out_specs=P(None, "row", None, None, "col", None),
        check_vma=False,
    )
```

```python
import functools

import jax
import jax.numpy as jnp
from jax import lax
from jax.experimental import pallas as pl
from jax.experimental.pallas import tpu as pltpu
from jax.sharding import PartitionSpec as P

BS = 128
NP = 8
GRID = 16
NX = 4
NZ = 8
RB = 8
HALF = RB * BS // 2
PAIRS = [(k, i) for k in range(NP) for i in range(k, NP)]
FIRST = [PAIRS.index((k, k)) for k in range(NP)]
DROWS = len(PAIRS) * BS
DCHUNK = DROWS // (2 * NZ)
MESH = pl.DeviceIdType.MESH
HIGHEST = lax.Precision.HIGHEST
SMEM = pl.BlockSpec(memory_space=pltpu.SMEM)
VMEM = pl.BlockSpec(memory_space=pltpu.VMEM)

T_POS, T_OWN, T_M1R, T_M2R, T_M1C, T_M2C, T_BNUM, T_KCOL, T_ROW, T_ROWN = range(0, 80, 8)


def table_kernel(slots_ref, first_ref, second_ref, tab_ref):
    own_row = lax.axis_index("row")
    own_col = lax.axis_index("col")
    for index in range(8):
        for base in (T_M1R, T_M2R, T_M1C, T_M2C):
            tab_ref[base + index] = 0
        tab_ref[T_BNUM + index] = NP
        tab_ref[T_KCOL + index] = NP
    for k in range(NP):
        slot = slots_ref[k]
        high, low = slot // GRID, slot % GRID
        tab_ref[T_POS + k] = high
        tab_ref[T_ROW + k] = high
        tab_ref[T_OWN + k] = (low == own_col).astype(jnp.int32)
        tab_ref[T_ROWN + k] = (low == own_row).astype(jnp.int32)

        @pl.when(low == own_col)
        def _():
            tab_ref[T_KCOL + high] = k

        @pl.when(low == own_row)
        def _():
            tab_ref[T_BNUM + high] = k

    for list_ref, base_row, base_col in ((first_ref, T_M1R, T_M1C), (second_ref, T_M2R, T_M2C)):

        def mark(entry, carry, list_ref=list_ref, base_row=base_row, base_col=base_col):
            slot = slots_ref[list_ref[entry]]
            high, low = slot // GRID, slot % GRID

            @pl.when(low == own_row)
            def _():
                tab_ref[base_row + high] = 1

            @pl.when(low == own_col)
            def _():
                tab_ref[base_col + high] = 1

            return carry

        lax.fori_loop(0, list_ref.shape[0], mark, 0)


def make_table(slots, first, second):
    return pl.pallas_call(
        table_kernel,
        out_shape=jax.ShapeDtypeStruct((80,), jnp.int32),
        in_specs=[SMEM] * 3,
        out_specs=SMEM,
        name="table",
    )(slots, first, second)


class Links:
    def __init__(self, send, recv):
        self.send, self.recv, self.used = send, recv, 0

    def copy(self, src, dst, row, col):
        op = pltpu.make_async_remote_copy(
            src_ref=src,
            dst_ref=dst,
            send_sem=self.send.at[self.used],
            recv_sem=self.recv.at[self.used],
            device_id=(row, col),
            device_id_type=MESH,
        )
        self.used += 1
        op.start()
        return op


def wait_all(ops):
    for op in ops:
        op.wait()


def gather_kernel(
    tab_ref, front_ref, vp_ref, vq_ref, l_ref, inv_ref, d, dc, vc, rc, d_pair, v_pair, d_ring, v_ring, r_ring, dx, send, recv
):
    p = lax.axis_index("row")
    q = lax.axis_index("col")
    x, y = p % NX, p // NX
    z, h = q // 2, q % 2
    other = 1 - h
    links = Links(send, recv)
    sibling = (p, q + 1 - 2 * h)
    zright = (p, (q + 2) % GRID)
    zleft = (p, (q + GRID - 2) % GRID)

    def at_x(d):
        return (y * NX + (x + d + NX) % NX, q)

    def at_y(d):
        return (((y + d + NX) % NX) * NX + x, q)

    partners = [sibling, zright, zleft] + [at_x(d) for d in (1, 2, 3)] + [at_y(d) for d in (1, 2, 3)]
    barrier = pltpu.get_barrier_semaphore()
    for row, col in partners:
        pl.semaphore_signal(barrier, inc=1, device_id=(row, col), device_id_type=MESH)

    def chunk(ref, rows, zz, hh, lo=0, size=None):
        size = rows if size is None else size
        return ref.at[pl.ds(pl.multiple_of((zz * 2 + hh) * rows + lo, 8), size), :]

    def pack_square():
        for index, (k, i) in enumerate(PAIRS):
            start = tab_ref[T_ROW + i] * (BS * RB) + tab_ref[T_POS + k]
            mine = tab_ref[T_OWN + k] * tab_ref[T_ROWN + i]
            block = front_ref[pl.ds(start, BS, RB), :]
            dc[pl.ds(index * BS, BS), :] = jnp.where(mine > 0, block, 0.0)

    def pack_panel(buf, flag, shift, step):
        def column(k, carry):
            start = tab_ref[shift + k] * (1 if shift == T_POS else BS * RB)
            mine = tab_ref[flag + k]

            def block(a, inner):
                value = front_ref[pl.ds(start + a * step, BS, RB), :]
                buf[pl.ds(pl.multiple_of((k * RB + a) * BS, BS), BS), :] = jnp.where(mine > 0, value, 0.0)
                return inner

            return lax.fori_loop(0, RB, block, carry)

        lax.fori_loop(0, NP, column, 0)

    def reduce_to_z(buf, rows, pair_buf, ring_buf):
        ops = []
        for zz in range(NZ):
            ops.append(links.copy(chunk(buf, rows, zz, other), pair_buf.at[pl.ds(zz * rows, rows), :], *sibling))
        yield
        wait_all(ops)

        def add_pair(zz, carry):
            target = chunk(buf, rows, zz, h)
            target[...] += pair_buf[pl.ds(pl.multiple_of(zz * rows, 8), rows), :]
            return carry

        lax.fori_loop(0, NZ, add_pair, 0)
        split = rows // 2
        for step in range(1, 5):
            far = 5 - step
            if step == 1:
                right = chunk(buf, rows, (z + 4) % NZ, h, 0, split)
                left = chunk(buf, rows, (z + 4) % NZ, h, split, split)
                to_right = ring_buf.at[0, step - 1, pl.ds(0, split), :]
                to_left = ring_buf.at[1, step - 1, pl.ds(split, split), :]
            else:
                right = chunk(buf, rows, (z + far) % NZ, h)
                left = chunk(buf, rows, (z + NZ - far) % NZ, h)
                to_right = ring_buf.at[0, step - 1]
                to_left = ring_buf.at[1, step - 1]
            ops = [links.copy(right, to_right, *zright), links.copy(left, to_left, *zleft)]
            yield
            wait_all(ops)
            for side, dest in ((0, (z + far - 1) % NZ), (1, (z + NZ - far + 1) % NZ)):
                lo, size = (0, rows) if step > 1 else (side * split, split)
                target = chunk(buf, rows, dest, h, lo, size)
                target[...] += ring_buf[side, step - 1, pl.ds(lo, size), :]

    def gather_z(buf, rows):
        pair = [links.copy(chunk(buf, rows, z, h), chunk(buf, rows, z, h), *sibling)]
        split = rows // 2
        for step in range(1, 5):
            ahead = (z + NZ - step + 1) % NZ
            behind = (z + step - 1) % NZ
            if step < 4:
                right = chunk(buf, rows, ahead, h)
                left = chunk(buf, rows, behind, h)
            else:
                right = chunk(buf, rows, ahead, h, 0, split)
                left = chunk(buf, rows, behind, h, split, split)
            ops = [links.copy(right, right, *zright), links.copy(left, left, *zleft)]
            yield
            wait_all(ops)
            got = [(z + NZ - step) % NZ, (z + step) % NZ][: 2 if step < 4 else 1]
            for zz in got:
                pair.append(links.copy(chunk(buf, rows, zz, h), chunk(buf, rows, zz, h), *sibling))
        yield
        wait_all(pair)

    def square():
        yield from reduce_to_z(dc, DCHUNK, d_pair, d_ring)
        quarter = DCHUNK // 4
        base = (z * 2 + h) * DCHUNK

        def part(ref, xx):
            return ref.at[pl.ds(pl.multiple_of(base + xx * quarter, 8), quarter), :]

        ops = [links.copy(part(dc, (x + s) % NX), dx.at[0, s - 1], *at_x(s)) for s in (1, 2, 3)]
        yield
        wait_all(ops)
        own = part(dc, x)
        own[...] += dx[0, 0] + dx[0, 1] + dx[0, 2]
        ops = [links.copy(own, dx.at[1, s - 1], *at_y(s)) for s in (1, 2, 3)]
        yield
        wait_all(ops)
        part(d, x)[...] = own[...] + (dx[1, 0] + dx[1, 1] + dx[1, 2])
        ops = [links.copy(part(d, x), part(d, x), *at_x(s)) for s in (1, 2, 3)]
        yield
        wait_all(ops)
        yield from gather_z(d, DCHUNK)

    def row_panel():
        yield from reduce_to_z(vc, HALF, v_pair, v_ring)
        chunk(vp_ref, HALF, z, h)[...] = chunk(vc, HALF, z, h)[...]
        yield from gather_z(vp_ref, HALF)

    lo, hi = HALF // 2, HALF // 4

    def xy_chunk(ref, axis, here, line, begin, size):
        xx, yy = (here, line) if axis == "x" else (line, here)
        return chunk(ref, HALF, yy * 2 + xx // 2, xx % 2, begin, size)

    def column_panel():
        for turn in (0, 1):
            sides = ((0, 0, "x"), (1, lo, "y")) if turn == 0 else ((0, 0, "y"), (1, lo, "x"))
            for step in (1, 2):
                ops, sums = [], []
                for half, begin, axis in sides:
                    me, across = (x, y) if axis == "x" else (y, x)
                    move = at_x if axis == "x" else at_y
                    lines = [(n, n) for n in range(NX)] if turn == 0 else [(NX, across)]
                    for side, way in ((0, 1), (1, NX - 1)):
                        for slot, line in lines:
                            if step == 1:
                                start, size, target, after = begin + side * hi, hi, (me + 2) % NX, (me + way) % NX
                            else:
                                start, size, target, after = begin, lo, (me + way) % NX, me
                            landing = r_ring.at[half, step - 1, side, slot, pl.ds(start - begin, size), :]
                            src = xy_chunk(rc, axis, target, line, start, size)
                            ops.append(links.copy(src, landing, *move(way)))
                            sums.append((xy_chunk(rc, axis, after, line, start, size), landing))
                yield
                wait_all(ops)
                for target, landing in sums:
                    target[...] += landing[...]
        for block in range(HALF // BS):
            source = chunk(rc, HALF, p // 2, p % 2, block * BS, BS)
            chunk(vq_ref, HALF, p // 2, p % 2, block * BS, BS)[...] = source[...].T
        for turn in (0, 1):
            sides = ((0, "x"), (lo, "y")) if turn == 0 else ((0, "y"), (lo, "x"))
            for step in (1, 2):
                ops = []
                for begin, axis in sides:
                    me, across = (x, y) if axis == "x" else (y, x)
                    move = at_x if axis == "x" else at_y
                    lines = [across] if turn == 0 else list(range(NX))
                    for side, way in ((0, 1), (1, NX - 1)):
                        for line in lines:
                            if step == 1:
                                start, size, origin = begin, lo, me
                            else:
                                start, size, origin = begin + side * hi, hi, (me + NX - way) % NX
                            ref = xy_chunk(vq_ref, axis, origin, line, start, size)
                            ops.append(links.copy(ref, ref, *move(way)))
                yield
                wait_all(ops)

    pack_square()
    pl.semaphore_wait(barrier, len(partners))
    first, rows, cols = square(), row_panel(), column_panel()
    next(first)
    pack_panel(rc, T_ROWN, T_ROW, 1)
    next(cols)
    pack_panel(vc, T_OWN, T_POS, BS * RB)
    for mark in "ddcdddcdcddcdcdcd":
        next(first if mark == "d" else cols)
    next(rows)
    for op in first:
        pass
    for k in range(NP):
        next(rows)
        if k < 3:
            next(cols, None)
        factor_step(k, d, l_ref, inv_ref)
    for op in cols:
        pass
    for op in rows:
        pass


def gather_and_factor(table, front):
    copies = 160
    panel = jax.ShapeDtypeStruct((GRID * HALF, BS), jnp.float32)
    return pl.pallas_call(
        gather_kernel,
        out_shape=[
            panel,
            panel,
            jax.ShapeDtypeStruct((DROWS, BS), jnp.float32),
            jax.ShapeDtypeStruct((NP, BS, BS), jnp.float32),
        ],
        in_specs=[SMEM, VMEM],
        out_specs=[VMEM] * 4,
        scratch_shapes=[
            pltpu.VMEM((DROWS, BS), jnp.float32),
            pltpu.VMEM((DROWS, BS), jnp.float32),
            pltpu.VMEM((GRID * HALF, BS), jnp.float32),
            pltpu.VMEM((GRID * HALF, BS), jnp.float32),
            pltpu.VMEM((DROWS // 2, BS), jnp.float32),
            pltpu.VMEM((GRID * HALF // 2, BS), jnp.float32),
            pltpu.VMEM((2, 4, DCHUNK, BS), jnp.float32),
            pltpu.VMEM((2, 4, HALF, BS), jnp.float32),
            pltpu.VMEM((2, 2, 2, NX + 1, HALF // 2, BS), jnp.float32),
            pltpu.VMEM((2, 3, DCHUNK // 4, BS), jnp.float32),
            pltpu.SemaphoreType.DMA((copies,)),
            pltpu.SemaphoreType.DMA((copies,)),
        ],
        compiler_params=pltpu.CompilerParams(
            collective_id=0, has_side_effects=True, vmem_limit_bytes=56 * 2**20
        ),
        name="gather_and_factor",
    )(table, front)


def row_of(value, index):
    return jnp.broadcast_to(value[index : index + 1, :], value.shape)


def eliminate(rows, extra, step):
    sub = lax.broadcasted_iota(jnp.int32, (8, BS), 0)
    cols = [jnp.broadcast_to(rows[:, 8 * step + c : 8 * step + c + 1], (8, BS)) for c in range(8)]
    pivots = jnp.zeros((8, BS), jnp.float32)
    for c in range(8):
        pivot = row_of(cols[c], c)
        mult = jnp.where(sub > c, cols[c] * (1.0 / pivot), 0.0)
        pivots = jnp.where(sub == c, pivot, pivots)
        for later in range(c + 1, 8):
            cols[later] = cols[later] - mult * row_of(cols[later], c)
        rows = rows - mult * row_of(rows, c)
        extra = extra - mult * row_of(extra, c)
    scale = lax.rsqrt(pivots)
    return rows * scale, extra * scale


def factor_block(block):
    row = lax.broadcasted_iota(jnp.int32, (BS, BS), 0)
    col = lax.broadcasted_iota(jnp.int32, (BS, BS), 1)
    lane = lax.broadcasted_iota(jnp.int32, (8, BS), 1)
    work = jnp.concatenate([block, (row == col).astype(jnp.float32)], axis=1)
    upper, inverse = [], []
    for step in range(BS // 8):
        rows, extra = eliminate(work[:8, :BS], work[:8, BS:], step)
        rows = jnp.where(lane >= 8 * step, rows, 0.0)
        upper.append(rows)
        inverse.append(extra)
        if step < BS // 8 - 1:
            work = work[8:]
            both = jnp.concatenate([rows, extra], axis=1)
            turned = rows.T[8 * step + 8 :]
            for c in range(8):
                work = work - jnp.broadcast_to(turned[:, c : c + 1], work.shape) * jnp.broadcast_to(
                    both[c : c + 1, :], work.shape
                )
    upper = jnp.concatenate(upper, axis=0)
    return jnp.where(col >= row, upper, 0.0), jnp.concatenate(inverse, axis=0)


def dot_nt(a, b, precision=HIGHEST):
    return lax.dot_general(a, b, (((1,), (1,)), ((), ())), precision=precision, preferred_element_type=jnp.float32)


def factor_step(k, work, l_ref, inv_ref):
    top = FIRST[k] * BS
    upper, inverse = factor_block(work[pl.ds(top, BS), :])
    l_ref[pl.ds(top, BS), :] = upper.T
    inv_ref[k] = inverse
    if k == NP - 1:
        return
    below = dot_nt(work[pl.ds(top + BS, (NP - 1 - k) * BS), :], inverse)
    l_ref[pl.ds(top + BS, (NP - 1 - k) * BS), :] = below
    for j in range(k + 1, NP):
        part = below[(j - k - 1) * BS :]
        rows = pl.ds(FIRST[j] * BS, (NP - j) * BS)
        work[rows, :] -= dot_nt(part, part[:BS])


def split(value):
    high = value.astype(jnp.bfloat16)
    return high, (value - high.astype(jnp.float32)).astype(jnp.bfloat16)


def dot3(a, b):
    (ah, al), (bh, bl) = a, b
    dims = (((1,), (1,)), ((), ()))
    mm = functools.partial(lax.dot_general, dimension_numbers=dims, preferred_element_type=jnp.float32)
    return mm(ah, bh) + (mm(ah, bl) + mm(al, bh))


WIDE = 2 * BS
TILE = 256


def update_kernel(tab_ref, front_ref, vp_ref, vq_ref, l_ref, inv_ref, out_ref, sh, sl, sf, lh, ll, ih, il):
    def block(i, k):
        return l_ref[pl.ds((FIRST[k] + i - k) * BS, BS), :]

    zero = jnp.zeros((BS, BS), jnp.float32)
    for wide in range(NP // 2):
        a, b = 2 * wide, 2 * wide + 1
        cross = -lax.dot_general(
            inv_ref[b],
            lax.dot_general(block(b, a), inv_ref[a], (((1,), (0,)), ((), ())), precision=HIGHEST),
            (((1,), (0,)), ((), ())),
            precision=HIGHEST,
        )
        inverse = jnp.concatenate(
            [jnp.concatenate([inv_ref[a], zero], axis=1), jnp.concatenate([cross, inv_ref[b]], axis=1)], axis=0
        )
        ih[wide], il[wide] = split(inverse)
        for before in range(wide):
            c, d = 2 * before, 2 * before + 1
            piece = jnp.concatenate(
                [
                    jnp.concatenate([block(a, c), block(a, d)], axis=1),
                    jnp.concatenate([block(b, c), block(b, d)], axis=1),
                ],
                axis=0,
            )
            rows, cols = pl.ds(wide * WIDE, WIDE), pl.ds(before * WIDE, WIDE)
            lh[rows, cols], ll[rows, cols] = split(piece)

    for part, (v_ref, first, second) in enumerate(((vp_ref, T_M1R, T_M2R), (vq_ref, T_M1C, T_M2C))):

        def solve(t, carry, part=part, v_ref=v_ref, first=first, second=second):
            low = t * TILE
            rows = pl.ds(pl.multiple_of(part * RB * BS + low, TILE), TILE)
            which = lax.broadcasted_iota(jnp.int32, (TILE, WIDE), 0) // BS
            keep = []
            for base in (first, second):
                even, odd = tab_ref[base + 2 * t], tab_ref[base + 2 * t + 1]
                keep.append(jnp.where(which == 0, even, odd) > 0)
            for wide in range(NP // 2):
                raw = jnp.concatenate(
                    [
                        v_ref[pl.ds(pl.multiple_of(k * RB * BS + low, TILE), TILE), :]
                        for k in (2 * wide, 2 * wide + 1)
                    ],
                    axis=1,
                )
                if wide:
                    old = pl.ds(0, wide * WIDE)
                    down = pl.ds(wide * WIDE, WIDE)
                    raw = raw - dot3((sh[rows, old], sl[rows, old]), (lh[down, old], ll[down, old]))
                solved = dot3(split(raw), (ih[wide], il[wide]))
                solved = jnp.where(keep[wide // 2], solved, 0.0)
                cols = pl.ds(wide * WIDE, WIDE)
                sh[rows, cols], sl[rows, cols] = split(solved)
                if part == 0:
                    for k in (2 * wide, 2 * wide + 1):
                        sf[k, pl.ds(pl.multiple_of(low, TILE), TILE), :] = solved[:, (k % 2) * BS : (k % 2 + 1) * BS]
            return carry

        lax.fori_loop(0, RB * BS // TILE, solve, 0)

    for t in range(RB * BS // TILE):
        rows = pl.ds(t * TILE, TILE)

        def update(u, carry, t=t, rows=rows):
            cols = pl.ds(pl.multiple_of(RB * BS + u * WIDE, WIDE), WIDE)
            term = dot3((sh[rows, :], sl[rows, :]), (sh[cols, :], sl[cols, :]))
            for a in range(2):
                for b in range(2):
                    row_block, col_block = 2 * t + a, 2 * u + b
                    place = pl.ds(row_block * BS * RB + col_block, BS, RB)
                    out_ref[place, :] = front_ref[place, :] - term[a * BS : (a + 1) * BS, b * BS : (b + 1) * BS]
            return carry

        lax.fori_loop(0, RB // 2, update, 0)

    for k in range(NP):
        base = T_M1R if k < NP // 2 else T_M2R

        @pl.when(tab_ref[T_OWN + k] > 0)
        def _():
            for a in range(RB):
                place = pl.ds(a * BS * RB + tab_ref[T_POS + k], BS, RB)
                number = tab_ref[T_BNUM + a]

                @pl.when((number >= NP) & (tab_ref[base + a] > 0))
                def _():
                    out_ref[place, :] = sf[k, pl.ds(a * BS, BS), :]

                @pl.when((number < NP) & ((number >= NP // 2) | (k < NP // 2)))
                def _():
                    start = (FIRST[k] + jnp.maximum(number - k, 0)) * BS
                    piece = l_ref[pl.ds(pl.multiple_of(start, BS), BS), :]
                    out_ref[place, :] = jnp.where(number >= k, piece, 0.0)


def update(table, front, vp, vq, lower, inverses):
    order = NP * BS
    return pl.pallas_call(
        update_kernel,
        out_shape=jax.ShapeDtypeStruct(front.shape, jnp.float32),
        in_specs=[SMEM] + [VMEM] * 5,
        out_specs=VMEM,
        scratch_shapes=[
            pltpu.VMEM((2 * RB * BS, order), jnp.bfloat16),
            pltpu.VMEM((2 * RB * BS, order), jnp.bfloat16),
            pltpu.VMEM((NP, RB * BS, BS), jnp.float32),
            pltpu.VMEM((order, order), jnp.bfloat16),
            pltpu.VMEM((order, order), jnp.bfloat16),
            pltpu.VMEM((NP // 2, WIDE, WIDE), jnp.bfloat16),
            pltpu.VMEM((NP // 2, WIDE, WIDE), jnp.bfloat16),
        ],
        compiler_params=pltpu.CompilerParams(vmem_limit_bytes=60 * 2**20),
        name="update",
    )(table, front, vp, vq, lower, inverses)


def on_device(front, block_slots, rows_first, rows_second):
    table = make_table(block_slots, rows_first, rows_second)
    flat = front.reshape(RB * BS * RB, BS)
    vp, vq, lower, inverses = gather_and_factor(table, flat)
    return update(table, flat, vp, vq, lower, inverses).reshape(front.shape)


def solution(mesh):
    placed = (P(None, "row", None, None, "col", None), P(), P(), P())
    return jax.shard_map(
        on_device,
        mesh=mesh,
        in_specs=placed,
        out_specs=P(None, "row", None, None, "col", None),
        check_vma=False,
    )
```

```python
import functools

import jax
import jax.numpy as jnp
from jax import lax
from jax.experimental import pallas as pl
from jax.experimental.pallas import tpu as pltpu
from jax.sharding import PartitionSpec as P

BS = 128
NP = 8
GRID = 16
NX = 4
NZ = 8
RB = 8
HALF = RB * BS // 2
PAIRS = [(k, i) for k in range(NP) for i in range(k, NP)]
FIRST = [PAIRS.index((k, k)) for k in range(NP)]
DROWS = len(PAIRS) * BS
DCHUNK = DROWS // (2 * NZ)
MESH = pl.DeviceIdType.MESH
HIGHEST = lax.Precision.HIGHEST
SMEM = pl.BlockSpec(memory_space=pltpu.SMEM)
VMEM = pl.BlockSpec(memory_space=pltpu.VMEM)


class Links:
    def __init__(self, send, recv):
        self.send, self.recv, self.used = send, recv, 0

    def copy(self, src, dst, row, col):
        op = pltpu.make_async_remote_copy(
            src_ref=src,
            dst_ref=dst,
            send_sem=self.send.at[self.used],
            recv_sem=self.recv.at[self.used],
            device_id=(row, col),
            device_id_type=MESH,
        )
        self.used += 1
        op.start()
        return op


def wait_all(ops):
    for op in ops:
        op.wait()


def gather_kernel(
    slots_ref, front_ref, vp_ref, vq_ref, l_ref, inv_ref, d, dc, vc, rc, d_pair, v_pair, d_ring, v_ring, r_ring, dx, send, recv
):
    p = lax.axis_index("row")
    q = lax.axis_index("col")
    x, y = p % NX, p // NX
    z, h = q // 2, q % 2
    other = 1 - h
    links = Links(send, recv)
    sibling = (p, q + 1 - 2 * h)
    zright = (p, (q + 2) % GRID)
    zleft = (p, (q + GRID - 2) % GRID)

    def at_x(d):
        return (y * NX + (x + d + NX) % NX, q)

    def at_y(d):
        return (((y + d + NX) % NX) * NX + x, q)

    partners = [sibling, zright, zleft] + [at_x(d) for d in (1, 2, 3)] + [at_y(d) for d in (1, 2, 3)]
    barrier = pltpu.get_barrier_semaphore()
    for row, col in partners:
        pl.semaphore_signal(barrier, inc=1, device_id=(row, col), device_id_type=MESH)

    def chunk(ref, rows, zz, hh, lo=0, size=None):
        size = rows if size is None else size
        return ref.at[pl.ds(pl.multiple_of((zz * 2 + hh) * rows + lo, 8), size), :]

    slots = [slots_ref[k] for k in range(NP)]
    high = [slot // GRID for slot in slots]
    low = [slot % GRID for slot in slots]

    def pack_square():
        for index, (k, i) in enumerate(PAIRS):
            block = front_ref[pl.ds(high[i] * (BS * RB) + high[k], BS, RB), :]
            dc[pl.ds(index * BS, BS), :] = jnp.where((low[k] == q) & (low[i] == p), block, 0.0)

    def pack_panel(buf, columns):
        def panel(k, carry):
            slot = slots_ref[k]
            mine = slot % GRID == (q if columns else p)
            start = slot // GRID * (1 if columns else BS * RB)

            def block(a, inner):
                value = front_ref[pl.ds(start + a * (BS * RB if columns else 1), BS, RB), :]
                buf[pl.ds(pl.multiple_of((k * RB + a) * BS, BS), BS), :] = jnp.where(mine, value, 0.0)
                return inner

            return lax.fori_loop(0, RB, block, carry)

        lax.fori_loop(0, NP, panel, 0)

    def reduce_to_z(buf, rows, pair_buf, ring_buf, pieces):
        ops = []
        for zz in range(NZ):
            ops.append(links.copy(chunk(buf, rows, zz, other), pair_buf.at[pl.ds(zz * rows, rows), :], *sibling))
        yield
        wait_all(ops)

        def add_pair(zz, carry):
            target = chunk(buf, rows, zz, h)
            target[...] += pair_buf[pl.ds(pl.multiple_of(zz * rows, 8), rows), :]
            return carry

        lax.fori_loop(0, NZ, add_pair, 0)
        split, size = rows // 2, rows // pieces
        flying = {}

        def land(key):
            op, side, step, lo, size = flying.pop(key)
            op.wait()
            dest = (z + 4 - step) % NZ if side == 0 else (z + NZ - 4 + step) % NZ
            target = chunk(buf, rows, dest, h, lo, size)
            target[...] += ring_buf[side, step - 1, pl.ds(lo, size), :]

        for step in range(1, 5):
            far = 5 - step
            for piece in range(pieces):
                for side, dest, way in ((0, (z + far) % NZ, zright), (1, (z + NZ - far) % NZ, zleft)):
                    if (side, piece) in flying:
                        land((side, piece))
                    lo, count = piece * size, size
                    if step == 1:
                        lo, count = side * split, split
                        if piece != side * (pieces - 1):
                            continue
                    src = chunk(buf, rows, dest, h, lo, count)
                    op = links.copy(src, ring_buf.at[side, step - 1, pl.ds(lo, count), :], *way)
                    flying[side, piece] = (op, side, step, lo, count)
            yield
        for key in list(flying):
            land(key)

    def gather_z(buf, rows, pieces):
        pair = [links.copy(chunk(buf, rows, z, h), chunk(buf, rows, z, h), *sibling)]
        size = rows // pieces
        split = rows // 2
        flying = {}

        def land(key):
            op, side, step, lo, size = flying.pop(key)
            op.wait()
            here = (z + NZ - step) % NZ if side == 0 else (z + step) % NZ
            part = chunk(buf, rows, here, h, lo, size)
            pair.append(links.copy(part, part, *sibling))

        for step in range(1, 5):
            for piece in range(pieces):
                for side, origin, way in ((0, (z + NZ - step + 1) % NZ, zright), (1, (z + step - 1) % NZ, zleft)):
                    if (side, piece) in flying:
                        land((side, piece))
                    lo, count = piece * size, size
                    if step == 4:
                        lo, count = side * split, split
                        if piece != side * (pieces - 1):
                            continue
                    part = chunk(buf, rows, origin, h, lo, count)
                    flying[side, piece] = (links.copy(part, part, *way), side, step, lo, count)
            yield
        for key in list(flying):
            land(key)
        yield
        wait_all(pair)

    def square():
        yield from reduce_to_z(dc, DCHUNK, d_pair, d_ring, 2)
        quarter = DCHUNK // 4
        base = (z * 2 + h) * DCHUNK

        def part(ref, xx):
            return ref.at[pl.ds(pl.multiple_of(base + xx * quarter, 8), quarter), :]

        ops = [links.copy(part(dc, (x + s) % NX), dx.at[0, s - 1], *at_x(s)) for s in (1, 2, 3)]
        yield
        wait_all(ops)
        own = part(dc, x)
        own[...] += dx[0, 0] + dx[0, 1] + dx[0, 2]
        ops = [links.copy(own, dx.at[1, s - 1], *at_y(s)) for s in (1, 2, 3)]
        yield
        wait_all(ops)
        part(d, x)[...] = own[...] + (dx[1, 0] + dx[1, 1] + dx[1, 2])
        ops = [links.copy(part(d, x), part(d, x), *at_x(s)) for s in (1, 2, 3)]
        yield
        wait_all(ops)
        yield from gather_z(d, DCHUNK, 2)

    def row_panel():
        yield from reduce_to_z(vc, HALF, v_pair, v_ring, 1)
        chunk(vp_ref, HALF, z, h)[...] = chunk(vc, HALF, z, h)[...]
        yield from gather_z(vp_ref, HALF, 1)

    lo, hi = HALF // 2, HALF // 4

    def xy_chunk(ref, axis, here, line, begin, size):
        xx, yy = (here, line) if axis == "x" else (line, here)
        return chunk(ref, HALF, yy * 2 + xx // 2, xx % 2, begin, size)

    def column_panel():
        for turn in (0, 1):
            sides = ((0, 0, "x"), (1, lo, "y")) if turn == 0 else ((0, 0, "y"), (1, lo, "x"))
            for step in (1, 2):
                ops, sums = [], []
                for half, begin, axis in sides:
                    me, across = (x, y) if axis == "x" else (y, x)
                    move = at_x if axis == "x" else at_y
                    lines = [(n, n) for n in range(NX)] if turn == 0 else [(NX, across)]
                    for side, way in ((0, 1), (1, NX - 1)):
                        for slot, line in lines:
                            if step == 1:
                                start, size, target, after = begin + side * hi, hi, (me + 2) % NX, (me + way) % NX
                            else:
                                start, size, target, after = begin, lo, (me + way) % NX, me
                            landing = r_ring.at[half, step - 1, side, slot, pl.ds(start - begin, size), :]
                            src = xy_chunk(rc, axis, target, line, start, size)
                            ops.append(links.copy(src, landing, *move(way)))
                            sums.append((xy_chunk(rc, axis, after, line, start, size), landing))
                yield
                wait_all(ops)
                for target, landing in sums:
                    target[...] += landing[...]
        for block in range(HALF // BS):
            source = chunk(rc, HALF, p // 2, p % 2, block * BS, BS)
            chunk(vq_ref, HALF, p // 2, p % 2, block * BS, BS)[...] = source[...].T
        for turn in (0, 1):
            sides = ((0, "x"), (lo, "y")) if turn == 0 else ((0, "y"), (lo, "x"))
            for step in (1, 2):
                ops = []
                for begin, axis in sides:
                    me, across = (x, y) if axis == "x" else (y, x)
                    move = at_x if axis == "x" else at_y
                    lines = [across] if turn == 0 else list(range(NX))
                    for side, way in ((0, 1), (1, NX - 1)):
                        for line in lines:
                            if step == 1:
                                start, size, origin = begin, lo, me
                            else:
                                start, size, origin = begin + side * hi, hi, (me + NX - way) % NX
                            ref = xy_chunk(vq_ref, axis, origin, line, start, size)
                            ops.append(links.copy(ref, ref, *move(way)))
                yield
                wait_all(ops)

    pack_square()
    pl.semaphore_wait(barrier, len(partners))
    work = {"d": square(), "r": row_panel(), "c": column_panel()}

    def go(marks):
        for mark in marks:
            next(work[mark], None)

    go("d")
    pack_panel(rc, False)
    go("cd")
    pack_panel(vc, True)
    go("rdcddrdrdcddcdcdcdrdd")
    between = ["", "c", "r", "c", "c", "r", "", ""]
    middle = ["r", "", "", "r", "", "", "r", ""]
    for k in range(NP):
        go(between[k])
        factor_step(k, d, l_ref, inv_ref, functools.partial(go, middle[k]))
    for key in "cr":
        for op in work[key]:
            pass


def gather_and_factor(slots, front):
    copies = 192
    panel = jax.ShapeDtypeStruct((GRID * HALF, BS), jnp.float32)
    return pl.pallas_call(
        gather_kernel,
        out_shape=[
            panel,
            panel,
            jax.ShapeDtypeStruct((DROWS, BS), jnp.float32),
            jax.ShapeDtypeStruct((NP, BS, BS), jnp.float32),
        ],
        in_specs=[SMEM, VMEM],
        out_specs=[VMEM] * 4,
        scratch_shapes=[
            pltpu.VMEM((DROWS, BS), jnp.float32),
            pltpu.VMEM((DROWS, BS), jnp.float32),
            pltpu.VMEM((GRID * HALF, BS), jnp.float32),
            pltpu.VMEM((GRID * HALF, BS), jnp.float32),
            pltpu.VMEM((DROWS // 2, BS), jnp.float32),
            pltpu.VMEM((GRID * HALF // 2, BS), jnp.float32),
            pltpu.VMEM((2, 4, DCHUNK, BS), jnp.float32),
            pltpu.VMEM((2, 4, HALF, BS), jnp.float32),
            pltpu.VMEM((2, 2, 2, NX + 1, HALF // 2, BS), jnp.float32),
            pltpu.VMEM((2, 3, DCHUNK // 4, BS), jnp.float32),
            pltpu.SemaphoreType.DMA((copies,)),
            pltpu.SemaphoreType.DMA((copies,)),
        ],
        compiler_params=pltpu.CompilerParams(
            collective_id=0, has_side_effects=True, vmem_limit_bytes=56 * 2**20
        ),
        name="gather_and_factor",
    )(slots, front)


def row_of(value, index):
    return jnp.broadcast_to(value[index : index + 1, :], value.shape)


def thirds(value):
    high = value.astype(jnp.bfloat16)
    rest = value - high.astype(jnp.float32)
    middle = rest.astype(jnp.bfloat16)
    return high, middle, (rest - middle.astype(jnp.float32)).astype(jnp.bfloat16)


def factor_block(block):
    row = lax.broadcasted_iota(jnp.int32, (BS, BS), 0)
    col = lax.broadcasted_iota(jnp.int32, (BS, BS), 1)
    lane = lax.broadcasted_iota(jnp.int32, (8, BS), 1)
    sub = lax.broadcasted_iota(jnp.int32, (8, BS), 0)
    identity = (row == col).astype(jnp.float32)
    steps = BS // 8
    left = [block[8 * t : 8 * t + 8] for t in range(steps)]
    right = [identity[8 * t : 8 * t + 8] for t in range(steps)]
    upper, inverse = [], []
    for s in range(steps):
        more = s + 1 < steps
        rows, extra = left[s], right[s]
        cols = [jnp.broadcast_to(rows[:, 8 * s + c : 8 * s + c + 1], (8, BS)) for c in range(8)]
        if more:
            rows2, extra2 = left[s + 1], right[s + 1]
            cols2 = [jnp.broadcast_to(rows2[:, 8 * s + c : 8 * s + c + 1], (8, BS)) for c in range(8)]
        pivots = jnp.zeros((8, BS), jnp.float32)
        for c in range(8):
            pivot = row_of(cols[c], c)
            recip = 1.0 / pivot
            mult = jnp.where(sub > c, cols[c] * recip, 0.0)
            pivots = jnp.where(sub == c, pivot, pivots)
            row_left, row_right = row_of(rows, c), row_of(extra, c)
            if more:
                mult2 = cols2[c] * recip
            for later in range(c + 1, 8):
                entry = row_of(cols[later], c)
                cols[later] = cols[later] - mult * entry
                if more:
                    cols2[later] = cols2[later] - mult2 * entry
            rows = rows - mult * row_left
            extra = extra - mult * row_right
            if more:
                rows2 = rows2 - mult2 * row_left
                extra2 = extra2 - mult2 * row_right
        scale = lax.rsqrt(pivots)
        rows = jnp.where(lane >= 8 * s, rows * scale, 0.0)
        extra = extra * scale
        upper.append(rows)
        inverse.append(extra)
        if more:
            left[s + 1], right[s + 1] = rows2, extra2
        if s + 2 < steps:
            high, middle, low = thirds(jnp.concatenate([rows, extra], axis=1))
            a = jnp.concatenate([v[:, :BS] for v in (high, high, middle, high, low, middle)], axis=0)
            b = jnp.concatenate([high, middle, high, low, high, middle], axis=0)
            term = lax.dot_general(a, b, (((0,), (0,)), ((), ())), preferred_element_type=jnp.float32)
            for t in range(s + 2, steps):
                left[t] = left[t] - term[8 * t : 8 * t + 8, :BS]
                right[t] = right[t] - term[8 * t : 8 * t + 8, BS:]
    upper = jnp.concatenate(upper, axis=0)
    return jnp.where(col >= row, upper, 0.0), jnp.concatenate(inverse, axis=0)


def dot_nt(a, b, precision=HIGHEST):
    return lax.dot_general(a, b, (((1,), (1,)), ((), ())), precision=precision, preferred_element_type=jnp.float32)


def factor_step(k, work, l_ref, inv_ref, middle):
    top = FIRST[k] * BS
    upper, inverse = factor_block(work[pl.ds(top, BS), :])
    middle()
    l_ref[pl.ds(top, BS), :] = upper.T
    inv_ref[k] = inverse
    if k == NP - 1:
        return
    below = dot_nt(work[pl.ds(top + BS, (NP - 1 - k) * BS), :], inverse)
    l_ref[pl.ds(top + BS, (NP - 1 - k) * BS), :] = below
    for j in range(k + 1, NP):
        part = below[(j - k - 1) * BS :]
        rows = pl.ds(FIRST[j] * BS, (NP - j) * BS)
        work[rows, :] -= dot_nt(part, part[:BS])


def split(value):
    high = value.astype(jnp.bfloat16)
    return high, (value - high.astype(jnp.float32)).astype(jnp.bfloat16)


def dot3(a, b):
    (ah, al), (bh, bl) = a, b
    dims = (((1,), (1,)), ((), ()))
    mm = functools.partial(lax.dot_general, dimension_numbers=dims, preferred_element_type=jnp.float32)
    return mm(ah, bh) + (mm(ah, bl) + mm(al, bh))


WIDE = 2 * BS


def update_kernel(
    slots_ref, first_ref, second_ref, front_ref, vp_ref, vq_ref, l_ref, inv_ref, out_ref, sh, sl, sf, lh, ll, ih, il
):
    def block(i, k):
        return l_ref[pl.ds((FIRST[k] + i - k) * BS, BS), :]

    zero = jnp.zeros((BS, BS), jnp.float32)
    for wide in range(NP // 2):
        a, b = 2 * wide, 2 * wide + 1
        cross = -lax.dot_general(
            inv_ref[b],
            lax.dot_general(block(b, a), inv_ref[a], (((1,), (0,)), ((), ())), precision=HIGHEST),
            (((1,), (0,)), ((), ())),
            precision=HIGHEST,
        )
        inverse = jnp.concatenate(
            [jnp.concatenate([inv_ref[a], zero], axis=1), jnp.concatenate([cross, inv_ref[b]], axis=1)], axis=0
        )
        ih[wide], il[wide] = split(inverse)
        for before in range(wide):
            c, d = 2 * before, 2 * before + 1
            piece = jnp.concatenate(
                [
                    jnp.concatenate([block(a, c), block(a, d)], axis=1),
                    jnp.concatenate([block(b, c), block(b, d)], axis=1),
                ],
                axis=0,
            )
            rows, cols = pl.ds(wide * WIDE, WIDE), pl.ds(before * WIDE, WIDE)
            lh[rows, cols], ll[rows, cols] = split(piece)

    p = lax.axis_index("row")
    q = lax.axis_index("col")
    marks = []
    for list_ref in (first_ref, second_ref):

        def mark(entry, carry, list_ref=list_ref):
            slot = slots_ref[list_ref[entry]]
            bit = jnp.left_shift(1, slot // GRID)
            low = slot % GRID
            return (
                carry[0] | jnp.where(low == p, bit, 0),
                carry[1] | jnp.where(low == q, bit, 0),
            )

        marks.append(lax.fori_loop(0, list_ref.shape[0], mark, (jnp.int32(0), jnp.int32(0))))

    def listed(panel, part, index):
        return jnp.bitwise_and(jnp.right_shift(marks[panel][part], index), 1) > 0

    order = RB * BS
    for wide in range(NP // 2):
        for part, v_ref in enumerate((vp_ref, vq_ref)):
            rows = pl.ds(part * order, order)
            cols = pl.ds(wide * WIDE, WIDE)
            raw = jnp.concatenate([v_ref[pl.ds(k * order, order), :] for k in (2 * wide, 2 * wide + 1)], axis=1)
            if wide:
                old = pl.ds(0, wide * WIDE)
                raw = raw - dot3((sh[rows, old], sl[rows, old]), (lh[cols, old], ll[cols, old]))
            solved = dot3(split(raw), (ih[wide], il[wide]))
            for a in range(RB):
                piece = jnp.where(listed(2 * wide // (NP // 2), part, a), solved[a * BS : (a + 1) * BS], 0.0)
                place = pl.ds(part * order + a * BS, BS)
                sh[place, cols], sl[place, cols] = split(piece)
                if part == 0:
                    for k in (2 * wide, 2 * wide + 1):
                        sf[k, pl.ds(a * BS, BS), :] = piece[:, (k % 2) * BS : (k % 2 + 1) * BS]

    def update(u, carry):
        rows = pl.ds(0, order)
        cols = pl.ds(pl.multiple_of(order + u * WIDE, WIDE), WIDE)
        term = dot3((sh[rows, :], sl[rows, :]), (sh[cols, :], sl[cols, :]))
        for a in range(RB):
            for b in range(2):
                place = pl.ds(a * BS * RB + 2 * u + b, BS, RB)
                out_ref[place, :] = front_ref[place, :] - term[a * BS : (a + 1) * BS, b * BS : (b + 1) * BS]
        return carry

    lax.fori_loop(0, RB // 2, update, 0)

    for k in range(NP):
        slot = slots_ref[k]

        @pl.when(slot % GRID == q)
        def _():
            for a in range(RB):
                place = pl.ds(a * BS * RB + slot // GRID, BS, RB)
                number = jnp.int32(NP)
                for i in range(NP):
                    number = jnp.where(slots_ref[i] == a * GRID + p, i, number)

                @pl.when((number >= NP) & listed(k // (NP // 2), 0, a))
                def _():
                    out_ref[place, :] = sf[k, pl.ds(a * BS, BS), :]

                @pl.when((number < NP) & ((number >= NP // 2) | (k < NP // 2)))
                def _():
                    start = (FIRST[k] + jnp.maximum(number - k, 0)) * BS
                    piece = l_ref[pl.ds(pl.multiple_of(start, BS), BS), :]
                    out_ref[place, :] = jnp.where(number >= k, piece, 0.0)


def update(slots, first, second, front, vp, vq, lower, inverses):
    order = NP * BS
    return pl.pallas_call(
        update_kernel,
        out_shape=jax.ShapeDtypeStruct(front.shape, jnp.float32),
        in_specs=[SMEM] * 3 + [VMEM] * 5,
        out_specs=VMEM,
        scratch_shapes=[
            pltpu.VMEM((2 * RB * BS, order), jnp.bfloat16),
            pltpu.VMEM((2 * RB * BS, order), jnp.bfloat16),
            pltpu.VMEM((NP, RB * BS, BS), jnp.float32),
            pltpu.VMEM((order, order), jnp.bfloat16),
            pltpu.VMEM((order, order), jnp.bfloat16),
            pltpu.VMEM((NP // 2, WIDE, WIDE), jnp.bfloat16),
            pltpu.VMEM((NP // 2, WIDE, WIDE), jnp.bfloat16),
        ],
        compiler_params=pltpu.CompilerParams(vmem_limit_bytes=60 * 2**20),
        name="update",
    )(slots, first, second, front, vp, vq, lower, inverses)


def on_device(front, block_slots, rows_first, rows_second):
    flat = front.reshape(RB * BS * RB, BS)
    vp, vq, lower, inverses = gather_and_factor(block_slots, flat)
    return update(block_slots, rows_first, rows_second, flat, vp, vq, lower, inverses).reshape(front.shape)


def solution(mesh):
    placed = (P(None, "row", None, None, "col", None), P(), P(), P())
    return jax.shard_map(
        on_device,
        mesh=mesh,
        in_specs=placed,
        out_specs=P(None, "row", None, None, "col", None),
        check_vma=False,
    )
```

```python
import functools

import jax
import jax.numpy as jnp
from jax import lax
from jax.experimental import pallas as pl
from jax.experimental.pallas import tpu as pltpu
from jax.sharding import PartitionSpec as P

BS = 128
NP = 8
GRID = 16
NX = 4
NZ = 8
RB = 8
HALF = RB * BS // 2
PAIRS = [(k, i) for k in range(NP) for i in range(k, NP)]
FIRST = [PAIRS.index((k, k)) for k in range(NP)]
DROWS = len(PAIRS) * BS
DCHUNK = DROWS // (2 * NZ)
MESH = pl.DeviceIdType.MESH
HIGHEST = lax.Precision.HIGHEST
SMEM = pl.BlockSpec(memory_space=pltpu.SMEM)
VMEM = pl.BlockSpec(memory_space=pltpu.VMEM)
ANY = pl.BlockSpec(memory_space=pl.ANY)


class Links:
    def __init__(self, send, recv):
        self.send, self.recv, self.used = send, recv, 0

    def copy(self, src, dst, row, col):
        op = pltpu.make_async_remote_copy(
            src_ref=src,
            dst_ref=dst,
            send_sem=self.send.at[self.used],
            recv_sem=self.recv.at[self.used],
            device_id=(row, col),
            device_id_type=MESH,
        )
        self.used += 1
        op.start()
        return op


def wait_all(ops):
    for op in ops:
        op.wait()


def gather_kernel(
    slots_ref, front_ref, vp_ref, vq_ref, l_ref, inv_ref, d, dc, vc, rc, d_pair, v_pair, d_ring, v_ring, r_ring, dx, send, recv
):
    p = lax.axis_index("row")
    q = lax.axis_index("col")
    x, y = p % NX, p // NX
    z, h = q // 2, q % 2
    other = 1 - h
    links = Links(send, recv)
    sibling = (p, q + 1 - 2 * h)
    zright = (p, (q + 2) % GRID)
    zleft = (p, (q + GRID - 2) % GRID)

    def at_x(d):
        return (y * NX + (x + d + NX) % NX, q)

    def at_y(d):
        return (((y + d + NX) % NX) * NX + x, q)

    partners = [sibling, zright, zleft] + [at_x(d) for d in (1, 2, 3)] + [at_y(d) for d in (1, 2, 3)]
    barrier = pltpu.get_barrier_semaphore()
    for row, col in partners:
        pl.semaphore_signal(barrier, inc=1, device_id=(row, col), device_id_type=MESH)

    def chunk(ref, rows, zz, hh, lo=0, size=None):
        size = rows if size is None else size
        return ref.at[pl.ds(pl.multiple_of((zz * 2 + hh) * rows + lo, 8), size), :]

    slots = [slots_ref[k] for k in range(NP)]
    high = [slot // GRID for slot in slots]
    low = [slot % GRID for slot in slots]

    def pack_square():
        for index, (k, i) in enumerate(PAIRS):
            block = front_ref[pl.ds(high[i] * (BS * RB) + high[k], BS, RB), :]
            dc[pl.ds(index * BS, BS), :] = jnp.where((low[k] == q) & (low[i] == p), block, 0.0)

    def pack_panel(buf, columns):
        def panel(k, carry):
            slot = slots_ref[k]
            mine = slot % GRID == (q if columns else p)
            start = slot // GRID * (1 if columns else BS * RB)

            def block(a, inner):
                value = front_ref[pl.ds(start + a * (BS * RB if columns else 1), BS, RB), :]
                buf[pl.ds(pl.multiple_of((k * RB + a) * BS, BS), BS), :] = jnp.where(mine, value, 0.0)
                return inner

            return lax.fori_loop(0, RB, block, carry)

        lax.fori_loop(0, NP, panel, 0)

    def reduce_to_z(buf, rows, pair_buf, ring_buf, pieces):
        ops = []
        for zz in range(NZ):
            ops.append(links.copy(chunk(buf, rows, zz, other), pair_buf.at[pl.ds(zz * rows, rows), :], *sibling))
        yield
        wait_all(ops)

        def add_pair(zz, carry):
            target = chunk(buf, rows, zz, h)
            target[...] += pair_buf[pl.ds(pl.multiple_of(zz * rows, 8), rows), :]
            return carry

        lax.fori_loop(0, NZ, add_pair, 0)
        split, size = rows // 2, rows // pieces
        flying = {}

        def land(key):
            op, side, step, lo, size = flying.pop(key)
            op.wait()
            dest = (z + 4 - step) % NZ if side == 0 else (z + NZ - 4 + step) % NZ
            target = chunk(buf, rows, dest, h, lo, size)
            target[...] += ring_buf[side, step - 1, pl.ds(lo, size), :]

        for step in range(1, 5):
            far = 5 - step
            for piece in range(pieces):
                for side, dest, way in ((0, (z + far) % NZ, zright), (1, (z + NZ - far) % NZ, zleft)):
                    if (side, piece) in flying:
                        land((side, piece))
                    lo, count = piece * size, size
                    if step == 1:
                        lo, count = side * split, split
                        if piece != side * (pieces - 1):
                            continue
                    src = chunk(buf, rows, dest, h, lo, count)
                    op = links.copy(src, ring_buf.at[side, step - 1, pl.ds(lo, count), :], *way)
                    flying[side, piece] = (op, side, step, lo, count)
            yield
        for key in list(flying):
            land(key)

    def gather_z(buf, rows, pieces):
        pair = [links.copy(chunk(buf, rows, z, h), chunk(buf, rows, z, h), *sibling)]
        size = rows // pieces
        split = rows // 2
        flying = {}

        def land(key):
            op, side, step, lo, size = flying.pop(key)
            op.wait()
            here = (z + NZ - step) % NZ if side == 0 else (z + step) % NZ
            part = chunk(buf, rows, here, h, lo, size)
            pair.append(links.copy(part, part, *sibling))

        for step in range(1, 5):
            for piece in range(pieces):
                for side, origin, way in ((0, (z + NZ - step + 1) % NZ, zright), (1, (z + step - 1) % NZ, zleft)):
                    if (side, piece) in flying:
                        land((side, piece))
                    lo, count = piece * size, size
                    if step == 4:
                        lo, count = side * split, split
                        if piece != side * (pieces - 1):
                            continue
                    part = chunk(buf, rows, origin, h, lo, count)
                    flying[side, piece] = (links.copy(part, part, *way), side, step, lo, count)
            yield
        for key in list(flying):
            land(key)
        yield
        wait_all(pair)

    def square():
        yield from reduce_to_z(dc, DCHUNK, d_pair, d_ring, 2)
        quarter = DCHUNK // 4
        base = (z * 2 + h) * DCHUNK

        def part(ref, xx):
            return ref.at[pl.ds(pl.multiple_of(base + xx * quarter, 8), quarter), :]

        ops = [links.copy(part(dc, (x + s) % NX), dx.at[0, s - 1], *at_x(s)) for s in (1, 2, 3)]
        yield
        wait_all(ops)
        own = part(dc, x)
        own[...] += dx[0, 0] + dx[0, 1] + dx[0, 2]
        ops = [links.copy(own, dx.at[1, s - 1], *at_y(s)) for s in (1, 2, 3)]
        yield
        wait_all(ops)
        part(d, x)[...] = own[...] + (dx[1, 0] + dx[1, 1] + dx[1, 2])
        ops = [links.copy(part(d, x), part(d, x), *at_x(s)) for s in (1, 2, 3)]
        yield
        wait_all(ops)
        yield from gather_z(d, DCHUNK, 2)

    def row_panel():
        yield from reduce_to_z(vc, HALF, v_pair, v_ring, 1)
        chunk(vp_ref, HALF, z, h)[...] = chunk(vc, HALF, z, h)[...]
        yield from gather_z(vp_ref, HALF, 1)

    lo, hi = HALF // 2, HALF // 4

    def xy_chunk(ref, axis, here, line, begin, size):
        xx, yy = (here, line) if axis == "x" else (line, here)
        return chunk(ref, HALF, yy * 2 + xx // 2, xx % 2, begin, size)

    def column_panel():
        for turn in (0, 1):
            sides = ((0, 0, "x"), (1, lo, "y")) if turn == 0 else ((0, 0, "y"), (1, lo, "x"))
            for step in (1, 2):
                ops, sums = [], []
                for half, begin, axis in sides:
                    me, across = (x, y) if axis == "x" else (y, x)
                    move = at_x if axis == "x" else at_y
                    lines = [(n, n) for n in range(NX)] if turn == 0 else [(NX, across)]
                    for side, way in ((0, 1), (1, NX - 1)):
                        for slot, line in lines:
                            if step == 1:
                                start, size, target, after = begin + side * hi, hi, (me + 2) % NX, (me + way) % NX
                            else:
                                start, size, target, after = begin, lo, (me + way) % NX, me
                            landing = r_ring.at[half, step - 1, side, slot, pl.ds(start - begin, size), :]
                            src = xy_chunk(rc, axis, target, line, start, size)
                            ops.append(links.copy(src, landing, *move(way)))
                            sums.append((xy_chunk(rc, axis, after, line, start, size), landing))
                yield
                wait_all(ops)
                for target, landing in sums:
                    target[...] += landing[...]
        for block in range(HALF // BS):
            source = chunk(rc, HALF, p // 2, p % 2, block * BS, BS)
            chunk(vq_ref, HALF, p // 2, p % 2, block * BS, BS)[...] = source[...].T
        for turn in (0, 1):
            sides = ((0, "x"), (lo, "y")) if turn == 0 else ((0, "y"), (lo, "x"))
            for step in (1, 2):
                ops = []
                for begin, axis in sides:
                    me, across = (x, y) if axis == "x" else (y, x)
                    move = at_x if axis == "x" else at_y
                    lines = [across] if turn == 0 else list(range(NX))
                    for side, way in ((0, 1), (1, NX - 1)):
                        for line in lines:
                            if step == 1:
                                start, size, origin = begin, lo, me
                            else:
                                start, size, origin = begin + side * hi, hi, (me + NX - way) % NX
                            ref = xy_chunk(vq_ref, axis, origin, line, start, size)
                            ops.append(links.copy(ref, ref, *move(way)))
                yield
                wait_all(ops)

    pack_square()
    pl.semaphore_wait(barrier, len(partners))
    work = {"d": square(), "r": row_panel(), "c": column_panel()}

    def go(marks):
        for mark in marks:
            next(work[mark], None)

    go("d")
    pack_panel(rc, False)
    go("cd")
    pack_panel(vc, True)
    go("rdcddrdrdcddcdcdcdrdd")
    between = ["", "c", "r", "c", "c", "r", "", ""]
    middle = ["r", "", "", "r", "", "", "r", ""]
    fill = []
    for k in range(NP):
        go(between[k])
        fill = factor_step(k, d, l_ref, inv_ref, fill, functools.partial(go, middle[k]))
    for key in "cr":
        for op in work[key]:
            pass


def gather_and_factor(slots, front):
    copies = 192
    panel = jax.ShapeDtypeStruct((GRID * HALF, BS), jnp.float32)
    return pl.pallas_call(
        gather_kernel,
        out_shape=[
            panel,
            panel,
            jax.ShapeDtypeStruct((DROWS, BS), jnp.float32),
            jax.ShapeDtypeStruct((NP, BS, BS), jnp.float32),
        ],
        in_specs=[SMEM, VMEM],
        out_specs=[VMEM] * 4,
        scratch_shapes=[
            pltpu.VMEM((DROWS, BS), jnp.float32),
            pltpu.VMEM((DROWS, BS), jnp.float32),
            pltpu.VMEM((GRID * HALF, BS), jnp.float32),
            pltpu.VMEM((GRID * HALF, BS), jnp.float32),
            pltpu.VMEM((DROWS // 2, BS), jnp.float32),
            pltpu.VMEM((GRID * HALF // 2, BS), jnp.float32),
            pltpu.VMEM((2, 4, DCHUNK, BS), jnp.float32),
            pltpu.VMEM((2, 4, HALF, BS), jnp.float32),
            pltpu.VMEM((2, 2, 2, NX + 1, HALF // 2, BS), jnp.float32),
            pltpu.VMEM((2, 3, DCHUNK // 4, BS), jnp.float32),
            pltpu.SemaphoreType.DMA((copies,)),
            pltpu.SemaphoreType.DMA((copies,)),
        ],
        compiler_params=pltpu.CompilerParams(
            collective_id=0, has_side_effects=True, vmem_limit_bytes=56 * 2**20
        ),
        name="gather_and_factor",
    )(slots, front)


def row_of(value, index):
    return jnp.broadcast_to(value[index : index + 1, :], value.shape)


def thirds(value):
    high = value.astype(jnp.bfloat16)
    rest = value - high.astype(jnp.float32)
    middle = rest.astype(jnp.bfloat16)
    return high, middle, (rest - middle.astype(jnp.float32)).astype(jnp.bfloat16)


def factor_block(block, fill):
    row = lax.broadcasted_iota(jnp.int32, (BS, BS), 0)
    col = lax.broadcasted_iota(jnp.int32, (BS, BS), 1)
    lane = lax.broadcasted_iota(jnp.int32, (8, BS), 1)
    sub = lax.broadcasted_iota(jnp.int32, (8, BS), 0)
    identity = (row == col).astype(jnp.float32)
    steps = BS // 8
    left = [block[8 * t : 8 * t + 8] for t in range(steps)]
    right = [identity[8 * t : 8 * t + 8] for t in range(steps)]
    upper, inverse = [], []
    for s in range(steps):
        more = s + 1 < steps
        rows, extra = left[s], right[s]
        cols = [jnp.broadcast_to(rows[:, 8 * s + c : 8 * s + c + 1], (8, BS)) for c in range(8)]
        if more:
            rows2, extra2 = left[s + 1], right[s + 1]
            cols2 = [jnp.broadcast_to(rows2[:, 8 * s + c : 8 * s + c + 1], (8, BS)) for c in range(8)]
        pivots = jnp.zeros((8, BS), jnp.float32)
        for c in range(8):
            pivot = row_of(cols[c], c)
            recip = 1.0 / pivot
            mult = jnp.where(sub > c, cols[c] * recip, 0.0)
            pivots = jnp.where(sub == c, pivot, pivots)
            row_left, row_right = row_of(rows, c), row_of(extra, c)
            if more:
                mult2 = cols2[c] * recip
            for later in range(c + 1, 8):
                entry = row_of(cols[later], c)
                cols[later] = cols[later] - mult * entry
                if more:
                    cols2[later] = cols2[later] - mult2 * entry
            rows = rows - mult * row_left
            extra = extra - mult * row_right
            if more:
                rows2 = rows2 - mult2 * row_left
                extra2 = extra2 - mult2 * row_right
        scale = lax.rsqrt(pivots)
        rows = jnp.where(lane >= 8 * s, rows * scale, 0.0)
        extra = extra * scale
        upper.append(rows)
        inverse.append(extra)
        if more:
            left[s + 1], right[s + 1] = rows2, extra2
        for piece in fill[s::steps]:
            piece()
        if s + 2 < steps:
            high, middle, low = thirds(jnp.concatenate([rows, extra], axis=1))
            a = jnp.concatenate([v[:, :BS] for v in (high, high, middle, high, low, middle)], axis=0)
            b = jnp.concatenate([high, middle, high, low, high, middle], axis=0)
            term = lax.dot_general(a, b, (((0,), (0,)), ((), ())), preferred_element_type=jnp.float32)
            for t in range(s + 2, steps):
                left[t] = left[t] - term[8 * t : 8 * t + 8, :BS]
                right[t] = right[t] - term[8 * t : 8 * t + 8, BS:]
    upper = jnp.concatenate(upper, axis=0)
    return jnp.where(col >= row, upper, 0.0), jnp.concatenate(inverse, axis=0)


def dot_nt(a, b, precision=HIGHEST):
    return lax.dot_general(a, b, (((1,), (1,)), ((), ())), precision=precision, preferred_element_type=jnp.float32)


def factor_step(k, work, l_ref, inv_ref, fill, middle):
    top = FIRST[k] * BS
    upper, inverse = factor_block(work[pl.ds(top, BS), :], fill)
    middle()
    l_ref[pl.ds(top, BS), :] = upper.T
    inv_ref[k] = inverse
    if k == NP - 1:
        return []
    first = dot_nt(work[pl.ds(top + BS, BS), :], inverse)
    l_ref[pl.ds(top + BS, BS), :] = first
    work[pl.ds(FIRST[k + 1] * BS, BS), :] -= dot_nt(first, first)

    def below():
        rows = pl.ds(top + 2 * BS, (NP - 2 - k) * BS)
        l_ref[rows, :] = dot_nt(work[rows, :], inv_ref[k])

    def later(i, j):
        def piece():
            a = l_ref[pl.ds(top + (i - k) * BS, (NP - i) * BS), :]
            b = l_ref[pl.ds(top + (j - k) * BS, BS), :]
            work[pl.ds((FIRST[j] + i - j) * BS, (NP - i) * BS), :] -= dot_nt(a, b)

        return piece

    if k == NP - 2:
        return []
    return [below] + [later(max(j, k + 2), j) for j in range(k + 1, NP)]


def split(value):
    high = value.astype(jnp.bfloat16)
    return high, (value - high.astype(jnp.float32)).astype(jnp.bfloat16)


def dot3(a, b):
    (ah, al), (bh, bl) = a, b
    dims = (((1,), (1,)), ((), ()))
    mm = functools.partial(lax.dot_general, dimension_numbers=dims, preferred_element_type=jnp.float32)
    return mm(ah, bh) + (mm(ah, bl) + mm(al, bh))


WIDE = 2 * BS


def update_kernel(
    slots_ref,
    first_ref,
    second_ref,
    front_hbm,
    vp_hbm,
    vq_hbm,
    l_ref,
    inv_ref,
    out_ref,
    front_ref,
    vp_ref,
    vq_ref,
    sh,
    sl,
    sf,
    lh,
    ll,
    ih,
    il,
    sem,
):
    order = RB * BS
    loads = []
    for wide in range(NP // 2):
        for part, (source, target) in enumerate(((vp_hbm, vp_ref), (vq_hbm, vq_ref))):
            rows = pl.ds(wide * 2 * order, 2 * order)
            loads.append(pltpu.make_async_copy(source.at[rows, :], target.at[rows, :], sem.at[len(loads)]))
    loads.append(pltpu.make_async_copy(front_hbm, front_ref, sem.at[len(loads)]))
    for load in loads:
        load.start()

    def block(i, k):
        return l_ref[pl.ds((FIRST[k] + i - k) * BS, BS), :]

    zero = jnp.zeros((BS, BS), jnp.float32)
    for wide in range(NP // 2):
        a, b = 2 * wide, 2 * wide + 1
        cross = -lax.dot_general(
            inv_ref[b],
            lax.dot_general(block(b, a), inv_ref[a], (((1,), (0,)), ((), ())), precision=HIGHEST),
            (((1,), (0,)), ((), ())),
            precision=HIGHEST,
        )
        inverse = jnp.concatenate(
            [jnp.concatenate([inv_ref[a], zero], axis=1), jnp.concatenate([cross, inv_ref[b]], axis=1)], axis=0
        )
        ih[wide], il[wide] = split(inverse)
        for before in range(wide):
            c, d = 2 * before, 2 * before + 1
            piece = jnp.concatenate(
                [
                    jnp.concatenate([block(a, c), block(a, d)], axis=1),
                    jnp.concatenate([block(b, c), block(b, d)], axis=1),
                ],
                axis=0,
            )
            rows, cols = pl.ds(wide * WIDE, WIDE), pl.ds(before * WIDE, WIDE)
            lh[rows, cols], ll[rows, cols] = split(piece)

    p = lax.axis_index("row")
    q = lax.axis_index("col")
    marks = []
    for list_ref in (first_ref, second_ref):

        def mark(entry, carry, list_ref=list_ref):
            slot = slots_ref[list_ref[entry]]
            bit = jnp.left_shift(1, slot // GRID)
            low = slot % GRID
            return (
                carry[0] | jnp.where(low == p, bit, 0),
                carry[1] | jnp.where(low == q, bit, 0),
            )

        marks.append(lax.fori_loop(0, list_ref.shape[0], mark, (jnp.int32(0), jnp.int32(0)), unroll=True))

    def listed(panel, part, index):
        return jnp.bitwise_and(jnp.right_shift(marks[panel][part], index), 1) > 0

    for wide in range(NP // 2):
        for part, v_ref in enumerate((vp_ref, vq_ref)):
            rows = pl.ds(part * order, order)
            cols = pl.ds(wide * WIDE, WIDE)
            loads[2 * wide + part].wait()
            raw = jnp.concatenate([v_ref[pl.ds(k * order, order), :] for k in (2 * wide, 2 * wide + 1)], axis=1)
            if wide:
                old = pl.ds(0, wide * WIDE)
                raw = raw - dot3((sh[rows, old], sl[rows, old]), (lh[cols, old], ll[cols, old]))
            solved = dot3(split(raw), (ih[wide], il[wide]))
            for a in range(RB):
                piece = jnp.where(listed(2 * wide // (NP // 2), part, a), solved[a * BS : (a + 1) * BS], 0.0)
                place = pl.ds(part * order + a * BS, BS)
                sh[place, cols], sl[place, cols] = split(piece)
                if part == 0:
                    for k in (2 * wide, 2 * wide + 1):
                        sf[k, pl.ds(a * BS, BS), :] = piece[:, (k % 2) * BS : (k % 2 + 1) * BS]

    loads[-1].wait()

    def update(u, carry):
        rows = pl.ds(0, order)
        cols = pl.ds(pl.multiple_of(order + u * WIDE, WIDE), WIDE)
        term = dot3((sh[rows, :], sl[rows, :]), (sh[cols, :], sl[cols, :]))
        for a in range(RB):
            for b in range(2):
                place = pl.ds(a * BS * RB + 2 * u + b, BS, RB)
                out_ref[place, :] = front_ref[place, :] - term[a * BS : (a + 1) * BS, b * BS : (b + 1) * BS]
        return carry

    lax.fori_loop(0, RB // 2, update, 0)

    for k in range(NP):
        slot = slots_ref[k]

        @pl.when(slot % GRID == q)
        def _():
            for a in range(RB):
                place = pl.ds(a * BS * RB + slot // GRID, BS, RB)
                number = jnp.int32(NP)
                for i in range(NP):
                    number = jnp.where(slots_ref[i] == a * GRID + p, i, number)

                @pl.when((number >= NP) & listed(k // (NP // 2), 0, a))
                def _():
                    out_ref[place, :] = sf[k, pl.ds(a * BS, BS), :]

                @pl.when((number < NP) & ((number >= NP // 2) | (k < NP // 2)))
                def _():
                    start = (FIRST[k] + jnp.maximum(number - k, 0)) * BS
                    piece = l_ref[pl.ds(pl.multiple_of(start, BS), BS), :]
                    out_ref[place, :] = jnp.where(number >= k, piece, 0.0)


def update(slots, first, second, front, vp, vq, lower, inverses):
    order = NP * BS
    return pl.pallas_call(
        update_kernel,
        out_shape=jax.ShapeDtypeStruct(front.shape, jnp.float32),
        in_specs=[SMEM] * 3 + [ANY] * 3 + [VMEM] * 2,
        out_specs=VMEM,
        scratch_shapes=[
            pltpu.VMEM(front.shape, jnp.float32),
            pltpu.VMEM(vp.shape, jnp.float32),
            pltpu.VMEM(vq.shape, jnp.float32),
            pltpu.VMEM((2 * RB * BS, order), jnp.bfloat16),
            pltpu.VMEM((2 * RB * BS, order), jnp.bfloat16),
            pltpu.VMEM((NP, RB * BS, BS), jnp.float32),
            pltpu.VMEM((order, order), jnp.bfloat16),
            pltpu.VMEM((order, order), jnp.bfloat16),
            pltpu.VMEM((NP // 2, WIDE, WIDE), jnp.bfloat16),
            pltpu.VMEM((NP // 2, WIDE, WIDE), jnp.bfloat16),
            pltpu.SemaphoreType.DMA((NP + 1,)),
        ],
        compiler_params=pltpu.CompilerParams(vmem_limit_bytes=60 * 2**20),
        name="update",
    )(slots, first, second, front, vp, vq, lower, inverses)


def on_device(front, block_slots, rows_first, rows_second):
    flat = front.reshape(RB * BS * RB, BS)
    vp, vq, lower, inverses = gather_and_factor(block_slots, flat)
    return update(block_slots, rows_first, rows_second, flat, vp, vq, lower, inverses).reshape(front.shape)


def solution(mesh):
    placed = (P(None, "row", None, None, "col", None), P(), P(), P())
    return jax.shard_map(
        on_device,
        mesh=mesh,
        in_specs=placed,
        out_specs=P(None, "row", None, None, "col", None),
        check_vma=False,
    )
```

```python
import functools

import jax
import jax.numpy as jnp
from jax import lax
from jax.experimental import pallas as pl
from jax.experimental.pallas import tpu as pltpu
from jax.sharding import PartitionSpec as P

BS = 128
NP = 8
GRID = 16
NX = 4
NZ = 8
RB = 8
HALF = RB * BS // 2
PAIRS = [(k, i) for k in range(NP) for i in range(k, NP)]
FIRST = [PAIRS.index((k, k)) for k in range(NP)]
DROWS = len(PAIRS) * BS
PB = NP // 2
ONE = [(k, i) for k in range(PB) for i in range(k, PB)]
TWO = [(k, i) for k in range(PB) for i in range(PB, NP)] + [(k, i) for k in range(PB, NP) for i in range(k, NP)]
BLOCKS_ONE, BLOCKS_TWO = 12, 28
MESH = pl.DeviceIdType.MESH
HIGHEST = lax.Precision.HIGHEST
SMEM = pl.BlockSpec(memory_space=pltpu.SMEM)
VMEM = pl.BlockSpec(memory_space=pltpu.VMEM)
ANY = pl.BlockSpec(memory_space=pl.ANY)


class Links:
    def __init__(self, send, recv):
        self.send, self.recv, self.used = send, recv, 0

    def copy(self, src, dst, row, col):
        op = pltpu.make_async_remote_copy(
            src_ref=src,
            dst_ref=dst,
            send_sem=self.send.at[self.used],
            recv_sem=self.recv.at[self.used],
            device_id=(row, col),
            device_id_type=MESH,
        )
        self.used += 1
        op.start()
        return op


def wait_all(ops):
    for op in ops:
        op.wait()


def gather_kernel(
    slots_ref, front_ref, vp_ref, vq_ref, l_ref, inv_ref, d1, d2, dc1, dc2, vc, rc,
    d_pair1, d_pair2, v_pair, d_ring1, d_ring2, v_ring, r_ring, dx1, dx2, send, recv
):
    p = lax.axis_index("row")
    q = lax.axis_index("col")
    x, y = p % NX, p // NX
    z, h = q // 2, q % 2
    other = 1 - h
    links = Links(send, recv)
    sibling = (p, q + 1 - 2 * h)
    zright = (p, (q + 2) % GRID)
    zleft = (p, (q + GRID - 2) % GRID)

    def at_x(d):
        return (y * NX + (x + d + NX) % NX, q)

    def at_y(d):
        return (((y + d + NX) % NX) * NX + x, q)

    partners = [sibling, zright, zleft] + [at_x(d) for d in (1, 2, 3)] + [at_y(d) for d in (1, 2, 3)]
    barrier = pltpu.get_barrier_semaphore()
    for row, col in partners:
        pl.semaphore_signal(barrier, inc=1, device_id=(row, col), device_id_type=MESH)

    def chunk(ref, rows, zz, hh, lo=0, size=None):
        size = rows if size is None else size
        return ref.at[pl.ds(pl.multiple_of((zz * 2 + hh) * rows + lo, 8), size), :]

    slots = [slots_ref[k] for k in range(NP)]
    high = [slot // GRID for slot in slots]
    low = [slot % GRID for slot in slots]

    def pack_square():
        for pairs, buf, blocks in ((ONE, dc1, BLOCKS_ONE), (TWO, dc2, BLOCKS_TWO)):
            for index, (k, i) in enumerate(pairs):
                block = front_ref[pl.ds(high[i] * (BS * RB) + high[k], BS, RB), :]
                buf[pl.ds(index * BS, BS), :] = jnp.where((low[k] == q) & (low[i] == p), block, 0.0)
            for index in range(len(pairs), blocks):
                buf[pl.ds(index * BS, BS), :] = jnp.zeros((BS, BS), jnp.float32)

    def pack_panel(buf, columns):
        def panel(k, carry):
            slot = slots_ref[k]
            mine = slot % GRID == (q if columns else p)
            start = slot // GRID * (1 if columns else BS * RB)

            def block(a, inner):
                value = front_ref[pl.ds(start + a * (BS * RB if columns else 1), BS, RB), :]
                buf[pl.ds(pl.multiple_of((k * RB + a) * BS, BS), BS), :] = jnp.where(mine, value, 0.0)
                return inner

            return lax.fori_loop(0, RB, block, carry)

        lax.fori_loop(0, NP, panel, 0)

    def reduce_to_z(buf, rows, pair_buf, ring_buf, pieces):
        ops = []
        for zz in range(NZ):
            ops.append(links.copy(chunk(buf, rows, zz, other), pair_buf.at[pl.ds(zz * rows, rows), :], *sibling))
        yield
        wait_all(ops)

        def add_pair(zz, carry):
            target = chunk(buf, rows, zz, h)
            target[...] += pair_buf[pl.ds(pl.multiple_of(zz * rows, 8), rows), :]
            return carry

        lax.fori_loop(0, NZ, add_pair, 0)
        split, size = rows // 2, rows // pieces
        flying = {}

        def land(key):
            op, side, step, lo, size = flying.pop(key)
            op.wait()
            dest = (z + 4 - step) % NZ if side == 0 else (z + NZ - 4 + step) % NZ
            target = chunk(buf, rows, dest, h, lo, size)
            target[...] += ring_buf[side, step - 1, pl.ds(lo, size), :]

        for step in range(1, 5):
            far = 5 - step
            for piece in range(pieces):
                for side, dest, way in ((0, (z + far) % NZ, zright), (1, (z + NZ - far) % NZ, zleft)):
                    if (side, piece) in flying:
                        land((side, piece))
                    lo, count = piece * size, size
                    if step == 1:
                        lo, count = side * split, split
                        if piece != side * (pieces - 1):
                            continue
                    src = chunk(buf, rows, dest, h, lo, count)
                    op = links.copy(src, ring_buf.at[side, step - 1, pl.ds(lo, count), :], *way)
                    flying[side, piece] = (op, side, step, lo, count)
            yield
        for key in list(flying):
            land(key)

    def gather_z(buf, rows, pieces):
        pair = [links.copy(chunk(buf, rows, z, h), chunk(buf, rows, z, h), *sibling)]
        size = rows // pieces
        split = rows // 2
        flying = {}

        def land(key):
            op, side, step, lo, size = flying.pop(key)
            op.wait()
            here = (z + NZ - step) % NZ if side == 0 else (z + step) % NZ
            part = chunk(buf, rows, here, h, lo, size)
            pair.append(links.copy(part, part, *sibling))

        for step in range(1, 5):
            for piece in range(pieces):
                for side, origin, way in ((0, (z + NZ - step + 1) % NZ, zright), (1, (z + step - 1) % NZ, zleft)):
                    if (side, piece) in flying:
                        land((side, piece))
                    lo, count = piece * size, size
                    if step == 4:
                        lo, count = side * split, split
                        if piece != side * (pieces - 1):
                            continue
                    part = chunk(buf, rows, origin, h, lo, count)
                    flying[side, piece] = (links.copy(part, part, *way), side, step, lo, count)
            yield
        for key in list(flying):
            land(key)
        yield
        wait_all(pair)

    def square(dc, d, pair_buf, ring_buf, dx, blocks, pieces):
        rows = blocks * BS // (2 * NZ)
        yield from reduce_to_z(dc, rows, pair_buf, ring_buf, pieces)
        quarter = rows // 4
        base = (z * 2 + h) * rows

        def part(ref, xx):
            return ref.at[pl.ds(pl.multiple_of(base + xx * quarter, 8), quarter), :]

        ops = [links.copy(part(dc, (x + s) % NX), dx.at[0, s - 1], *at_x(s)) for s in (1, 2, 3)]
        yield
        wait_all(ops)
        own = part(dc, x)
        own[...] += dx[0, 0] + dx[0, 1] + dx[0, 2]
        ops = [links.copy(own, dx.at[1, s - 1], *at_y(s)) for s in (1, 2, 3)]
        yield
        wait_all(ops)
        part(d, x)[...] = own[...] + (dx[1, 0] + dx[1, 1] + dx[1, 2])
        ops = [links.copy(part(d, x), part(d, x), *at_x(s)) for s in (1, 2, 3)]
        yield
        wait_all(ops)
        yield from gather_z(d, rows, pieces)

    def row_panel():
        yield from reduce_to_z(vc, HALF, v_pair, v_ring, 1)
        chunk(vp_ref, HALF, z, h)[...] = chunk(vc, HALF, z, h)[...]
        yield from gather_z(vp_ref, HALF, 1)

    lo, hi = HALF // 2, HALF // 4

    def xy_chunk(ref, axis, here, line, begin, size):
        xx, yy = (here, line) if axis == "x" else (line, here)
        return chunk(ref, HALF, yy * 2 + xx // 2, xx % 2, begin, size)

    def column_panel():
        for turn in (0, 1):
            sides = ((0, 0, "x"), (1, lo, "y")) if turn == 0 else ((0, 0, "y"), (1, lo, "x"))
            for step in (1, 2):
                ops, sums = [], []
                for half, begin, axis in sides:
                    me, across = (x, y) if axis == "x" else (y, x)
                    move = at_x if axis == "x" else at_y
                    lines = [(n, n) for n in range(NX)] if turn == 0 else [(NX, across)]
                    for side, way in ((0, 1), (1, NX - 1)):
                        for slot, line in lines:
                            if step == 1:
                                start, size, target, after = begin + side * hi, hi, (me + 2) % NX, (me + way) % NX
                            else:
                                start, size, target, after = begin, lo, (me + way) % NX, me
                            landing = r_ring.at[half, step - 1, side, slot, pl.ds(start - begin, size), :]
                            src = xy_chunk(rc, axis, target, line, start, size)
                            ops.append(links.copy(src, landing, *move(way)))
                            sums.append((xy_chunk(rc, axis, after, line, start, size), landing))
                yield
                wait_all(ops)
                for target, landing in sums:
                    target[...] += landing[...]
        for block in range(HALF // BS):
            source = chunk(rc, HALF, p // 2, p % 2, block * BS, BS)
            chunk(vq_ref, HALF, p // 2, p % 2, block * BS, BS)[...] = source[...].T
        for turn in (0, 1):
            sides = ((0, "x"), (lo, "y")) if turn == 0 else ((0, "y"), (lo, "x"))
            for step in (1, 2):
                ops = []
                for begin, axis in sides:
                    me, across = (x, y) if axis == "x" else (y, x)
                    move = at_x if axis == "x" else at_y
                    lines = [across] if turn == 0 else list(range(NX))
                    for side, way in ((0, 1), (1, NX - 1)):
                        for line in lines:
                            if step == 1:
                                start, size, origin = begin, lo, me
                            else:
                                start, size, origin = begin + side * hi, hi, (me + NX - way) % NX
                            ref = xy_chunk(vq_ref, axis, origin, line, start, size)
                            ops.append(links.copy(ref, ref, *move(way)))
                yield
                wait_all(ops)

    pack_square()
    pl.semaphore_wait(barrier, len(partners))
    work = {
        "1": square(dc1, d1, d_pair1, d_ring1, dx1, BLOCKS_ONE, 1),
        "2": square(dc2, d2, d_pair2, d_ring2, dx2, BLOCKS_TWO, 2),
        "r": row_panel(),
        "c": column_panel(),
    }

    def go(marks):
        for mark in marks:
            next(work[mark], None)

    go("12")
    pack_panel(rc, False)
    go("c1")
    pack_panel(vc, True)
    go("r1121c121212c1r2121" + "2c121r1")
    between = ["", "2", "r2", "rc", "c", "c", "rc", "r"]
    middle = ["2r", "2c", "2", "", "r", "", "", ""]
    factor(d1, d2, l_ref, inv_ref, lambda k: go(between[k]), lambda k: go(middle[k]))
    for key in "cr":
        for op in work[key]:
            pass


def gather_and_factor(slots, front):
    copies = 256
    panel = jax.ShapeDtypeStruct((GRID * HALF, BS), jnp.float32)
    return pl.pallas_call(
        gather_kernel,
        out_shape=[
            panel,
            panel,
            jax.ShapeDtypeStruct((DROWS, BS), jnp.float32),
            jax.ShapeDtypeStruct((NP, BS, BS), jnp.float32),
        ],
        in_specs=[SMEM, VMEM],
        out_specs=[VMEM] * 4,
        scratch_shapes=[
            pltpu.VMEM((BLOCKS_ONE * BS, BS), jnp.float32),
            pltpu.VMEM((BLOCKS_TWO * BS, BS), jnp.float32),
            pltpu.VMEM((BLOCKS_ONE * BS, BS), jnp.float32),
            pltpu.VMEM((BLOCKS_TWO * BS, BS), jnp.float32),
            pltpu.VMEM((GRID * HALF, BS), jnp.float32),
            pltpu.VMEM((GRID * HALF, BS), jnp.float32),
            pltpu.VMEM((BLOCKS_ONE * BS // 2, BS), jnp.float32),
            pltpu.VMEM((BLOCKS_TWO * BS // 2, BS), jnp.float32),
            pltpu.VMEM((GRID * HALF // 2, BS), jnp.float32),
            pltpu.VMEM((2, 4, BLOCKS_ONE * BS // (2 * NZ), BS), jnp.float32),
            pltpu.VMEM((2, 4, BLOCKS_TWO * BS // (2 * NZ), BS), jnp.float32),
            pltpu.VMEM((2, 4, HALF, BS), jnp.float32),
            pltpu.VMEM((2, 2, 2, NX + 1, HALF // 2, BS), jnp.float32),
            pltpu.VMEM((2, 3, BLOCKS_ONE * BS // (8 * NZ), BS), jnp.float32),
            pltpu.VMEM((2, 3, BLOCKS_TWO * BS // (8 * NZ), BS), jnp.float32),
            pltpu.SemaphoreType.DMA((copies,)),
            pltpu.SemaphoreType.DMA((copies,)),
        ],
        compiler_params=pltpu.CompilerParams(
            collective_id=0, has_side_effects=True, vmem_limit_bytes=56 * 2**20
        ),
        name="gather_and_factor",
    )(slots, front)


def row_of(value, index):
    return jnp.broadcast_to(value[index : index + 1, :], value.shape)


def thirds(value):
    high = value.astype(jnp.bfloat16)
    rest = value - high.astype(jnp.float32)
    middle = rest.astype(jnp.bfloat16)
    return high, middle, (rest - middle.astype(jnp.float32)).astype(jnp.bfloat16)


def factor_block(block, fill):
    row = lax.broadcasted_iota(jnp.int32, (BS, BS), 0)
    col = lax.broadcasted_iota(jnp.int32, (BS, BS), 1)
    lane = lax.broadcasted_iota(jnp.int32, (8, BS), 1)
    sub = lax.broadcasted_iota(jnp.int32, (8, BS), 0)
    identity = (row == col).astype(jnp.float32)
    steps = BS // 8
    left = [block[8 * t : 8 * t + 8] for t in range(steps)]
    right = [identity[8 * t : 8 * t + 8] for t in range(steps)]
    upper, inverse = [], []
    for s in range(steps):
        more = s + 1 < steps
        rows, extra = left[s], right[s]
        cols = [jnp.broadcast_to(rows[:, 8 * s + c : 8 * s + c + 1], (8, BS)) for c in range(8)]
        if more:
            rows2, extra2 = left[s + 1], right[s + 1]
            cols2 = [jnp.broadcast_to(rows2[:, 8 * s + c : 8 * s + c + 1], (8, BS)) for c in range(8)]
        pivots = jnp.zeros((8, BS), jnp.float32)
        for c in range(8):
            pivot = row_of(cols[c], c)
            recip = 1.0 / pivot
            mult = jnp.where(sub > c, cols[c] * recip, 0.0)
            pivots = jnp.where(sub == c, pivot, pivots)
            row_left, row_right = row_of(rows, c), row_of(extra, c)
            if more:
                mult2 = cols2[c] * recip
            for later in range(c + 1, 8):
                entry = row_of(cols[later], c)
                cols[later] = cols[later] - mult * entry
                if more:
                    cols2[later] = cols2[later] - mult2 * entry
            rows = rows - mult * row_left
            extra = extra - mult * row_right
            if more:
                rows2 = rows2 - mult2 * row_left
                extra2 = extra2 - mult2 * row_right
        scale = lax.rsqrt(pivots)
        rows = jnp.where(lane >= 8 * s, rows * scale, 0.0)
        extra = extra * scale
        upper.append(rows)
        inverse.append(extra)
        if more:
            left[s + 1], right[s + 1] = rows2, extra2
        for piece in fill[s::steps]:
            piece()
        if s + 2 < steps:
            high, middle, low = thirds(jnp.concatenate([rows, extra], axis=1))
            a = jnp.concatenate([v[:, :BS] for v in (high, high, middle, high, low, middle)], axis=0)
            b = jnp.concatenate([high, middle, high, low, high, middle], axis=0)
            term = lax.dot_general(a, b, (((0,), (0,)), ((), ())), preferred_element_type=jnp.float32)
            for t in range(s + 2, steps):
                left[t] = left[t] - term[8 * t : 8 * t + 8, :BS]
                right[t] = right[t] - term[8 * t : 8 * t + 8, BS:]
    upper = jnp.concatenate(upper, axis=0)
    return jnp.where(col >= row, upper, 0.0), jnp.concatenate(inverse, axis=0)


def dot_nt(a, b, precision=HIGHEST):
    return lax.dot_general(a, b, (((1,), (1,)), ((), ())), precision=precision, preferred_element_type=jnp.float32)


def factor(d1, d2, l_ref, inv_ref, between, middle):
    def place(k, i, count=1):
        ref, pairs = (d1, ONE) if i < PB else (d2, TWO)
        return ref.at[pl.ds(pairs.index((k, i)) * BS, count * BS), :]

    def done(k, i, count=1):
        return l_ref.at[pl.ds((FIRST[k] + i - k) * BS, count * BS), :]

    def cross(k):
        def piece():
            rows = place(k, PB, PB)[...]
            for j in range(k):
                rows = rows - dot_nt(done(j, PB, PB)[...], done(j, k)[...])
            done(k, PB, PB)[...] = dot_nt(rows, inv_ref[k])

        return piece

    def below(k, end):
        def piece():
            count = end - k - 2
            done(k, k + 2, count)[...] = dot_nt(place(k, k + 2, count)[...], inv_ref[k])

        return piece

    def later(panel, i, j, end):
        def piece():
            term = dot_nt(done(panel[0], i, end - i)[...], done(panel[0], j)[...])
            for k in panel[1:]:
                term = term + dot_nt(done(k, i, end - i)[...], done(k, j)[...])
            place(j, i, end - i)[...] -= term

        return piece

    fill = []
    for k in range(NP):
        end = PB if k < PB else NP
        between(k)
        if k == PB - 1:
            fill = fill + [cross(j) for j in range(PB - 1)]
        upper, inverse = factor_block(place(k, k)[...], fill)
        middle(k)
        done(k, k)[...] = upper.T
        inv_ref[k] = inverse
        fill = []
        if k == PB - 1:
            first = list(range(PB))
            cross(k)()
            term = dot_nt(done(0, PB)[...], done(0, PB)[...])
            for j in first[1:]:
                term = term + dot_nt(done(j, PB)[...], done(j, PB)[...])
            place(PB, PB)[...] -= term
            fill = [later(first, max(j, PB + 1), j, NP) for j in range(PB, NP)]
        elif k < end - 1:
            near = dot_nt(place(k, k + 1)[...], inverse)
            done(k, k + 1)[...] = near
            place(k + 1, k + 1)[...] -= dot_nt(near, near)
            if k < end - 2:
                fill = [below(k, end)] + [later([k], max(j, k + 2), j, end) for j in range(k + 1, end)]


def split(value):
    high = value.astype(jnp.bfloat16)
    return high, (value - high.astype(jnp.float32)).astype(jnp.bfloat16)


def dot3(a, b):
    (ah, al), (bh, bl) = a, b
    dims = (((1,), (1,)), ((), ()))
    mm = functools.partial(lax.dot_general, dimension_numbers=dims, preferred_element_type=jnp.float32)
    return mm(ah, bh) + (mm(ah, bl) + mm(al, bh))


WIDE = 2 * BS


def update_kernel(
    slots_ref,
    first_ref,
    second_ref,
    front_hbm,
    vp_hbm,
    vq_hbm,
    l_ref,
    inv_ref,
    out_ref,
    front_ref,
    vp_ref,
    vq_ref,
    sh,
    sl,
    sf,
    lh,
    ll,
    ih,
    il,
    sem,
):
    order = RB * BS
    loads = []
    for wide in range(NP // 2):
        for part, (source, target) in enumerate(((vp_hbm, vp_ref), (vq_hbm, vq_ref))):
            rows = pl.ds(wide * 2 * order, 2 * order)
            loads.append(pltpu.make_async_copy(source.at[rows, :], target.at[rows, :], sem.at[len(loads)]))
    loads.append(pltpu.make_async_copy(front_hbm, front_ref, sem.at[len(loads)]))
    for load in loads:
        load.start()

    def block(i, k):
        return l_ref[pl.ds((FIRST[k] + i - k) * BS, BS), :]

    zero = jnp.zeros((BS, BS), jnp.float32)
    for wide in range(NP // 2):
        a, b = 2 * wide, 2 * wide + 1
        cross = -lax.dot_general(
            inv_ref[b],
            lax.dot_general(block(b, a), inv_ref[a], (((1,), (0,)), ((), ())), precision=HIGHEST),
            (((1,), (0,)), ((), ())),
            precision=HIGHEST,
        )
        inverse = jnp.concatenate(
            [jnp.concatenate([inv_ref[a], zero], axis=1), jnp.concatenate([cross, inv_ref[b]], axis=1)], axis=0
        )
        ih[wide], il[wide] = split(inverse)
        for before in range(wide):
            c, d = 2 * before, 2 * before + 1
            piece = jnp.concatenate(
                [
                    jnp.concatenate([block(a, c), block(a, d)], axis=1),
                    jnp.concatenate([block(b, c), block(b, d)], axis=1),
                ],
                axis=0,
            )
            rows, cols = pl.ds(wide * WIDE, WIDE), pl.ds(before * WIDE, WIDE)
            lh[rows, cols], ll[rows, cols] = split(piece)

    p = lax.axis_index("row")
    q = lax.axis_index("col")
    marks = []
    for list_ref in (first_ref, second_ref):

        def mark(entry, carry, list_ref=list_ref):
            slot = slots_ref[list_ref[entry]]
            bit = jnp.left_shift(1, slot // GRID)
            low = slot % GRID
            return (
                carry[0] | jnp.where(low == p, bit, 0),
                carry[1] | jnp.where(low == q, bit, 0),
            )

        marks.append(lax.fori_loop(0, list_ref.shape[0], mark, (jnp.int32(0), jnp.int32(0)), unroll=True))

    def listed(panel, part, index):
        return jnp.bitwise_and(jnp.right_shift(marks[panel][part], index), 1) > 0

    for wide in range(NP // 2):
        for part, v_ref in enumerate((vp_ref, vq_ref)):
            rows = pl.ds(part * order, order)
            cols = pl.ds(wide * WIDE, WIDE)
            loads[2 * wide + part].wait()
            raw = jnp.concatenate([v_ref[pl.ds(k * order, order), :] for k in (2 * wide, 2 * wide + 1)], axis=1)
            if wide:
                old = pl.ds(0, wide * WIDE)
                raw = raw - dot3((sh[rows, old], sl[rows, old]), (lh[cols, old], ll[cols, old]))
            solved = dot3(split(raw), (ih[wide], il[wide]))
            for a in range(RB):
                piece = jnp.where(listed(2 * wide // (NP // 2), part, a), solved[a * BS : (a + 1) * BS], 0.0)
                place = pl.ds(part * order + a * BS, BS)
                sh[place, cols], sl[place, cols] = split(piece)
                if part == 0:
                    for k in (2 * wide, 2 * wide + 1):
                        sf[k, pl.ds(a * BS, BS), :] = piece[:, (k % 2) * BS : (k % 2 + 1) * BS]

    loads[-1].wait()

    def update(u, carry):
        rows = pl.ds(0, order)
        cols = pl.ds(pl.multiple_of(order + u * WIDE, WIDE), WIDE)
        term = dot3((sh[rows, :], sl[rows, :]), (sh[cols, :], sl[cols, :]))
        for a in range(RB):
            for b in range(2):
                place = pl.ds(a * BS * RB + 2 * u + b, BS, RB)
                out_ref[place, :] = front_ref[place, :] - term[a * BS : (a + 1) * BS, b * BS : (b + 1) * BS]
        return carry

    lax.fori_loop(0, RB // 2, update, 0)

    for k in range(NP):
        slot = slots_ref[k]

        @pl.when(slot % GRID == q)
        def _():
            for a in range(RB):
                place = pl.ds(a * BS * RB + slot // GRID, BS, RB)
                number = jnp.int32(NP)
                for i in range(NP):
                    number = jnp.where(slots_ref[i] == a * GRID + p, i, number)

                @pl.when((number >= NP) & listed(k // (NP // 2), 0, a))
                def _():
                    out_ref[place, :] = sf[k, pl.ds(a * BS, BS), :]

                @pl.when((number < NP) & ((number >= NP // 2) | (k < NP // 2)))
                def _():
                    start = (FIRST[k] + jnp.maximum(number - k, 0)) * BS
                    piece = l_ref[pl.ds(pl.multiple_of(start, BS), BS), :]
                    out_ref[place, :] = jnp.where(number >= k, piece, 0.0)


def update(slots, first, second, front, vp, vq, lower, inverses):
    order = NP * BS
    return pl.pallas_call(
        update_kernel,
        out_shape=jax.ShapeDtypeStruct(front.shape, jnp.float32),
        in_specs=[SMEM] * 3 + [ANY] * 3 + [VMEM] * 2,
        out_specs=VMEM,
        scratch_shapes=[
            pltpu.VMEM(front.shape, jnp.float32),
            pltpu.VMEM(vp.shape, jnp.float32),
            pltpu.VMEM(vq.shape, jnp.float32),
            pltpu.VMEM((2 * RB * BS, order), jnp.bfloat16),
            pltpu.VMEM((2 * RB * BS, order), jnp.bfloat16),
            pltpu.VMEM((NP, RB * BS, BS), jnp.float32),
            pltpu.VMEM((order, order), jnp.bfloat16),
            pltpu.VMEM((order, order), jnp.bfloat16),
            pltpu.VMEM((NP // 2, WIDE, WIDE), jnp.bfloat16),
            pltpu.VMEM((NP // 2, WIDE, WIDE), jnp.bfloat16),
            pltpu.SemaphoreType.DMA((NP + 1,)),
        ],
        compiler_params=pltpu.CompilerParams(vmem_limit_bytes=60 * 2**20),
        name="update",
    )(slots, first, second, front, vp, vq, lower, inverses)


def on_device(front, block_slots, rows_first, rows_second):
    flat = front.reshape(RB * BS * RB, BS)
    vp, vq, lower, inverses = gather_and_factor(block_slots, flat)
    return update(block_slots, rows_first, rows_second, flat, vp, vq, lower, inverses).reshape(front.shape)


def solution(mesh):
    placed = (P(None, "row", None, None, "col", None), P(), P(), P())
    return jax.shard_map(
        on_device,
        mesh=mesh,
        in_specs=placed,
        out_specs=P(None, "row", None, None, "col", None),
        check_vma=False,
    )
```

```python
import functools

import jax
import jax.numpy as jnp
from jax import lax
from jax.experimental import pallas as pl
from jax.experimental.pallas import tpu as pltpu
from jax.sharding import PartitionSpec as P

BS = 128
NP = 8
GRID = 16
NX = 4
NZ = 8
RB = 8
HALF = RB * BS // 2
PAIRS = [(k, i) for k in range(NP) for i in range(k, NP)]
FIRST = [PAIRS.index((k, k)) for k in range(NP)]
DROWS = len(PAIRS) * BS
DCHUNK = DROWS // (2 * NZ)
MESH = pl.DeviceIdType.MESH
HIGHEST = lax.Precision.HIGHEST
SMEM = pl.BlockSpec(memory_space=pltpu.SMEM)
VMEM = pl.BlockSpec(memory_space=pltpu.VMEM)
ANY = pl.BlockSpec(memory_space=pl.ANY)


class Links:
    def __init__(self, send, recv):
        self.send, self.recv, self.used = send, recv, 0

    def copy(self, src, dst, row, col):
        op = pltpu.make_async_remote_copy(
            src_ref=src,
            dst_ref=dst,
            send_sem=self.send.at[self.used],
            recv_sem=self.recv.at[self.used],
            device_id=(row, col),
            device_id_type=MESH,
        )
        self.used += 1
        op.start()
        return op


def wait_all(ops):
    for op in ops:
        op.wait()


def gather_kernel(
    slots_ref, front_ref, vp_ref, vq_hbm, l_ref, inv_ref, vq_ref, store_sem, d, dc, vc, rc, d_pair, v_pair, d_ring, v_ring, r_ring, dx, send, recv
):
    p = lax.axis_index("row")
    q = lax.axis_index("col")
    x, y = p % NX, p // NX
    z, h = q // 2, q % 2
    other = 1 - h
    links = Links(send, recv)
    sibling = (p, q + 1 - 2 * h)
    zright = (p, (q + 2) % GRID)
    zleft = (p, (q + GRID - 2) % GRID)

    def at_x(d):
        return (y * NX + (x + d + NX) % NX, q)

    def at_y(d):
        return (((y + d + NX) % NX) * NX + x, q)

    partners = [sibling, zright, zleft] + [at_x(d) for d in (1, 2, 3)] + [at_y(d) for d in (1, 2, 3)]
    barrier = pltpu.get_barrier_semaphore()
    for row, col in partners:
        pl.semaphore_signal(barrier, inc=1, device_id=(row, col), device_id_type=MESH)

    def chunk(ref, rows, zz, hh, lo=0, size=None):
        size = rows if size is None else size
        return ref.at[pl.ds(pl.multiple_of((zz * 2 + hh) * rows + lo, 8), size), :]

    slots = [slots_ref[k] for k in range(NP)]
    high = [slot // GRID for slot in slots]
    low = [slot % GRID for slot in slots]

    def pack_square():
        for index, (k, i) in enumerate(PAIRS):
            block = front_ref[pl.ds(high[i] * (BS * RB) + high[k], BS, RB), :]
            dc[pl.ds(index * BS, BS), :] = jnp.where((low[k] == q) & (low[i] == p), block, 0.0)

    def pack_panel(buf, columns):
        def panel(k, carry):
            slot = slots_ref[k]
            mine = slot % GRID == (q if columns else p)
            start = slot // GRID * (1 if columns else BS * RB)

            def block(a, inner):
                value = front_ref[pl.ds(start + a * (BS * RB if columns else 1), BS, RB), :]
                buf[pl.ds(pl.multiple_of((k * RB + a) * BS, BS), BS), :] = jnp.where(mine, value, 0.0)
                return inner

            return lax.fori_loop(0, RB, block, carry)

        lax.fori_loop(0, NP, panel, 0)

    def reduce_to_z(buf, rows, pair_buf, ring_buf, pieces):
        ops = []
        for zz in range(NZ):
            ops.append(links.copy(chunk(buf, rows, zz, other), pair_buf.at[pl.ds(zz * rows, rows), :], *sibling))
        yield
        wait_all(ops)

        def add_pair(zz, carry):
            target = chunk(buf, rows, zz, h)
            target[...] += pair_buf[pl.ds(pl.multiple_of(zz * rows, 8), rows), :]
            return carry

        lax.fori_loop(0, NZ, add_pair, 0)
        split, size = rows // 2, rows // pieces
        flying = {}

        def land(key):
            op, side, step, lo, size = flying.pop(key)
            op.wait()
            dest = (z + 4 - step) % NZ if side == 0 else (z + NZ - 4 + step) % NZ
            target = chunk(buf, rows, dest, h, lo, size)
            target[...] += ring_buf[side, step - 1, pl.ds(lo, size), :]

        for step in range(1, 5):
            far = 5 - step
            for piece in range(pieces):
                for side, dest, way in ((0, (z + far) % NZ, zright), (1, (z + NZ - far) % NZ, zleft)):
                    if (side, piece) in flying:
                        land((side, piece))
                    lo, count = piece * size, size
                    if step == 1:
                        lo, count = side * split, split
                        if piece != side * (pieces - 1):
                            continue
                    src = chunk(buf, rows, dest, h, lo, count)
                    op = links.copy(src, ring_buf.at[side, step - 1, pl.ds(lo, count), :], *way)
                    flying[side, piece] = (op, side, step, lo, count)
            yield
        for key in list(flying):
            land(key)

    def gather_z(buf, rows, pieces):
        pair = [links.copy(chunk(buf, rows, z, h), chunk(buf, rows, z, h), *sibling)]
        size = rows // pieces
        split = rows // 2
        flying = {}

        def land(key):
            op, side, step, lo, size = flying.pop(key)
            op.wait()
            here = (z + NZ - step) % NZ if side == 0 else (z + step) % NZ
            part = chunk(buf, rows, here, h, lo, size)
            pair.append(links.copy(part, part, *sibling))

        for step in range(1, 5):
            for piece in range(pieces):
                for side, origin, way in ((0, (z + NZ - step + 1) % NZ, zright), (1, (z + step - 1) % NZ, zleft)):
                    if (side, piece) in flying:
                        land((side, piece))
                    lo, count = piece * size, size
                    if step == 4:
                        lo, count = side * split, split
                        if piece != side * (pieces - 1):
                            continue
                    part = chunk(buf, rows, origin, h, lo, count)
                    flying[side, piece] = (links.copy(part, part, *way), side, step, lo, count)
            yield
        for key in list(flying):
            land(key)
        yield
        wait_all(pair)

    def square():
        yield from reduce_to_z(dc, DCHUNK, d_pair, d_ring, 2)
        quarter = DCHUNK // 4
        base = (z * 2 + h) * DCHUNK

        def part(ref, xx):
            return ref.at[pl.ds(pl.multiple_of(base + xx * quarter, 8), quarter), :]

        ops = [links.copy(part(dc, (x + s) % NX), dx.at[0, s - 1], *at_x(s)) for s in (1, 2, 3)]
        yield
        wait_all(ops)
        own = part(dc, x)
        own[...] += dx[0, 0] + dx[0, 1] + dx[0, 2]
        ops = [links.copy(own, dx.at[1, s - 1], *at_y(s)) for s in (1, 2, 3)]
        yield
        wait_all(ops)
        part(d, x)[...] = own[...] + (dx[1, 0] + dx[1, 1] + dx[1, 2])
        ops = [links.copy(part(d, x), part(d, x), *at_x(s)) for s in (1, 2, 3)]
        yield
        wait_all(ops)
        yield from gather_z(d, DCHUNK, 2)

    def row_panel():
        yield from reduce_to_z(vc, HALF, v_pair, v_ring, 1)
        chunk(vp_ref, HALF, z, h)[...] = chunk(vc, HALF, z, h)[...]
        yield from gather_z(vp_ref, HALF, 1)

    lo, hi = HALF // 2, HALF // 4

    def xy_chunk(ref, axis, here, line, begin, size):
        xx, yy = (here, line) if axis == "x" else (line, here)
        return chunk(ref, HALF, yy * 2 + xx // 2, xx % 2, begin, size)

    def column_panel():
        for turn in (0, 1):
            sides = ((0, 0, "x"), (1, lo, "y")) if turn == 0 else ((0, 0, "y"), (1, lo, "x"))
            for step in (1, 2):
                ops, sums = [], []
                for half, begin, axis in sides:
                    me, across = (x, y) if axis == "x" else (y, x)
                    move = at_x if axis == "x" else at_y
                    lines = [(n, n) for n in range(NX)] if turn == 0 else [(NX, across)]
                    for side, way in ((0, 1), (1, NX - 1)):
                        for slot, line in lines:
                            if step == 1:
                                start, size, target, after = begin + side * hi, hi, (me + 2) % NX, (me + way) % NX
                            else:
                                start, size, target, after = begin, lo, (me + way) % NX, me
                            landing = r_ring.at[half, step - 1, side, slot, pl.ds(start - begin, size), :]
                            src = xy_chunk(rc, axis, target, line, start, size)
                            ops.append(links.copy(src, landing, *move(way)))
                            sums.append((xy_chunk(rc, axis, after, line, start, size), landing))
                yield
                wait_all(ops)
                for target, landing in sums:
                    target[...] += landing[...]
        for block in range(HALF // BS):
            source = chunk(rc, HALF, p // 2, p % 2, block * BS, BS)
            chunk(vq_ref, HALF, p // 2, p % 2, block * BS, BS)[...] = source[...].T
        for turn in (0, 1):
            sides = ((0, "x"), (lo, "y")) if turn == 0 else ((0, "y"), (lo, "x"))
            for step in (1, 2):
                ops = []
                for begin, axis in sides:
                    me, across = (x, y) if axis == "x" else (y, x)
                    move = at_x if axis == "x" else at_y
                    lines = [across] if turn == 0 else list(range(NX))
                    for side, way in ((0, 1), (1, NX - 1)):
                        for line in lines:
                            if step == 1:
                                start, size, origin = begin, lo, me
                            else:
                                start, size, origin = begin + side * hi, hi, (me + NX - way) % NX
                            ref = xy_chunk(vq_ref, axis, origin, line, start, size)
                            ops.append(links.copy(ref, ref, *move(way)))
                yield
                wait_all(ops)

    pack_square()
    pl.semaphore_wait(barrier, len(partners))
    work = {"d": square(), "r": row_panel(), "c": column_panel()}

    def go(marks):
        for mark in marks:
            next(work[mark], None)

    go("d")
    pack_panel(rc, False)
    go("cd")
    pack_panel(vc, True)
    go("rdcddrdrdcddcdcdcdrdd")
    between = ["", "c", "r", "c", "c", "r", "", ""]
    middle = ["r", "", "", "r", "", "", "r", ""]
    fill = []
    store = pltpu.make_async_copy(vq_ref, vq_hbm, store_sem.at[0])
    for k in range(NP):
        go(between[k])
        if k == 4:
            for op in work["c"]:
                pass
            store.start()
        fill = factor_step(k, d, l_ref, inv_ref, fill, functools.partial(go, middle[k]))
    for op in work["r"]:
        pass
    store.wait()


def gather_and_factor(slots, front):
    copies = 192
    panel = jax.ShapeDtypeStruct((GRID * HALF, BS), jnp.float32)
    return pl.pallas_call(
        gather_kernel,
        out_shape=[
            panel,
            panel,
            jax.ShapeDtypeStruct((DROWS, BS), jnp.float32),
            jax.ShapeDtypeStruct((NP, BS, BS), jnp.float32),
        ],
        in_specs=[SMEM, VMEM],
        out_specs=[VMEM, ANY, VMEM, VMEM],
        scratch_shapes=[
            pltpu.VMEM((GRID * HALF, BS), jnp.float32),
            pltpu.SemaphoreType.DMA((1,)),
            pltpu.VMEM((DROWS, BS), jnp.float32),
            pltpu.VMEM((DROWS, BS), jnp.float32),
            pltpu.VMEM((GRID * HALF, BS), jnp.float32),
            pltpu.VMEM((GRID * HALF, BS), jnp.float32),
            pltpu.VMEM((DROWS // 2, BS), jnp.float32),
            pltpu.VMEM((GRID * HALF // 2, BS), jnp.float32),
            pltpu.VMEM((2, 4, DCHUNK, BS), jnp.float32),
            pltpu.VMEM((2, 4, HALF, BS), jnp.float32),
            pltpu.VMEM((2, 2, 2, NX + 1, HALF // 2, BS), jnp.float32),
            pltpu.VMEM((2, 3, DCHUNK // 4, BS), jnp.float32),
            pltpu.SemaphoreType.DMA((copies,)),
            pltpu.SemaphoreType.DMA((copies,)),
        ],
        compiler_params=pltpu.CompilerParams(
            collective_id=0, has_side_effects=True, vmem_limit_bytes=56 * 2**20
        ),
        name="gather_and_factor",
    )(slots, front)


def row_of(value, index):
    return jnp.broadcast_to(value[index : index + 1, :], value.shape)


def thirds(value):
    high = value.astype(jnp.bfloat16)
    rest = value - high.astype(jnp.float32)
    middle = rest.astype(jnp.bfloat16)
    return high, middle, (rest - middle.astype(jnp.float32)).astype(jnp.bfloat16)


def factor_block(block, fill):
    row = lax.broadcasted_iota(jnp.int32, (BS, BS), 0)
    col = lax.broadcasted_iota(jnp.int32, (BS, BS), 1)
    lane = lax.broadcasted_iota(jnp.int32, (8, BS), 1)
    sub = lax.broadcasted_iota(jnp.int32, (8, BS), 0)
    identity = (row == col).astype(jnp.float32)
    steps = BS // 8
    left = [block[8 * t : 8 * t + 8] for t in range(steps)]
    right = [identity[8 * t : 8 * t + 8] for t in range(steps)]
    upper, inverse = [], []
    for s in range(steps):
        more = s + 1 < steps
        rows, extra = left[s], right[s]
        cols = [jnp.broadcast_to(rows[:, 8 * s + c : 8 * s + c + 1], (8, BS)) for c in range(8)]
        if more:
            rows2, extra2 = left[s + 1], right[s + 1]
            cols2 = [jnp.broadcast_to(rows2[:, 8 * s + c : 8 * s + c + 1], (8, BS)) for c in range(8)]
        pivots = jnp.zeros((8, BS), jnp.float32)
        for c in range(8):
            pivot = row_of(cols[c], c)
            recip = 1.0 / pivot
            mult = jnp.where(sub > c, cols[c] * recip, 0.0)
            pivots = jnp.where(sub == c, pivot, pivots)
            row_left, row_right = row_of(rows, c), row_of(extra, c)
            if more:
                mult2 = cols2[c] * recip
            for later in range(c + 1, 8):
                entry = row_of(cols[later], c)
                cols[later] = cols[later] - mult * entry
                if more:
                    cols2[later] = cols2[later] - mult2 * entry
            rows = rows - mult * row_left
            extra = extra - mult * row_right
            if more:
                rows2 = rows2 - mult2 * row_left
                extra2 = extra2 - mult2 * row_right
        scale = lax.rsqrt(pivots)
        rows = jnp.where(lane >= 8 * s, rows * scale, 0.0)
        extra = extra * scale
        upper.append(rows)
        inverse.append(extra)
        if more:
            left[s + 1], right[s + 1] = rows2, extra2
        for piece in fill[s::steps]:
            piece()
        if s + 2 < steps:
            high, middle, low = thirds(jnp.concatenate([rows, extra], axis=1))
            a = jnp.concatenate([v[:, :BS] for v in (high, high, middle, high, low, middle)], axis=0)
            b = jnp.concatenate([high, middle, high, low, high, middle], axis=0)
            term = lax.dot_general(a, b, (((0,), (0,)), ((), ())), preferred_element_type=jnp.float32)
            for t in range(s + 2, steps):
                left[t] = left[t] - term[8 * t : 8 * t + 8, :BS]
                right[t] = right[t] - term[8 * t : 8 * t + 8, BS:]
    upper = jnp.concatenate(upper, axis=0)
    return jnp.where(col >= row, upper, 0.0), jnp.concatenate(inverse, axis=0)


def dot_nt(a, b, precision=HIGHEST):
    return lax.dot_general(a, b, (((1,), (1,)), ((), ())), precision=precision, preferred_element_type=jnp.float32)


def factor_step(k, work, l_ref, inv_ref, fill, middle):
    top = FIRST[k] * BS
    upper, inverse = factor_block(work[pl.ds(top, BS), :], fill)
    middle()
    l_ref[pl.ds(top, BS), :] = upper.T
    inv_ref[k] = inverse
    if k == NP - 1:
        return []
    first = dot_nt(work[pl.ds(top + BS, BS), :], inverse)
    l_ref[pl.ds(top + BS, BS), :] = first
    work[pl.ds(FIRST[k + 1] * BS, BS), :] -= dot_nt(first, first)

    def below():
        rows = pl.ds(top + 2 * BS, (NP - 2 - k) * BS)
        l_ref[rows, :] = dot_nt(work[rows, :], inv_ref[k])

    def later(i, j):
        def piece():
            a = l_ref[pl.ds(top + (i - k) * BS, (NP - i) * BS), :]
            b = l_ref[pl.ds(top + (j - k) * BS, BS), :]
            work[pl.ds((FIRST[j] + i - j) * BS, (NP - i) * BS), :] -= dot_nt(a, b)

        return piece

    if k == NP - 2:
        return []
    return [below] + [later(max(j, k + 2), j) for j in range(k + 1, NP)]


def split(value):
    high = value.astype(jnp.bfloat16)
    return high, (value - high.astype(jnp.float32)).astype(jnp.bfloat16)


def dot3(a, b):
    (ah, al), (bh, bl) = a, b
    dims = (((1,), (1,)), ((), ()))
    mm = functools.partial(lax.dot_general, dimension_numbers=dims, preferred_element_type=jnp.float32)
    return mm(ah, bh) + (mm(ah, bl) + mm(al, bh))


WIDE = 2 * BS


def update_kernel(
    slots_ref,
    first_ref,
    second_ref,
    front_hbm,
    vp_hbm,
    vq_hbm,
    l_ref,
    inv_ref,
    out_ref,
    front_ref,
    vp_ref,
    vq_ref,
    sh,
    sl,
    sf,
    lh,
    ll,
    ih,
    il,
    sem,
):
    order = RB * BS
    loads = []
    for wide in range(NP // 2):
        for part, (source, target) in enumerate(((vp_hbm, vp_ref), (vq_hbm, vq_ref))):
            rows = pl.ds(wide * 2 * order, 2 * order)
            loads.append(pltpu.make_async_copy(source.at[rows, :], target.at[rows, :], sem.at[len(loads)]))
    loads.append(pltpu.make_async_copy(front_hbm, front_ref, sem.at[len(loads)]))
    for load in loads:
        load.start()

    def block(i, k):
        return l_ref[pl.ds((FIRST[k] + i - k) * BS, BS), :]

    zero = jnp.zeros((BS, BS), jnp.float32)
    for wide in range(NP // 2):
        a, b = 2 * wide, 2 * wide + 1
        cross = -lax.dot_general(
            inv_ref[b],
            lax.dot_general(block(b, a), inv_ref[a], (((1,), (0,)), ((), ())), precision=HIGHEST),
            (((1,), (0,)), ((), ())),
            precision=HIGHEST,
        )
        inverse = jnp.concatenate(
            [jnp.concatenate([inv_ref[a], zero], axis=1), jnp.concatenate([cross, inv_ref[b]], axis=1)], axis=0
        )
        ih[wide], il[wide] = split(inverse)
        for before in range(wide):
            c, d = 2 * before, 2 * before + 1
            piece = jnp.concatenate(
                [
                    jnp.concatenate([block(a, c), block(a, d)], axis=1),
                    jnp.concatenate([block(b, c), block(b, d)], axis=1),
                ],
                axis=0,
            )
            rows, cols = pl.ds(wide * WIDE, WIDE), pl.ds(before * WIDE, WIDE)
            lh[rows, cols], ll[rows, cols] = split(piece)

    p = lax.axis_index("row")
    q = lax.axis_index("col")
    marks = []
    for list_ref in (first_ref, second_ref):

        def mark(entry, carry, list_ref=list_ref):
            slot = slots_ref[list_ref[entry]]
            bit = jnp.left_shift(1, slot // GRID)
            low = slot % GRID
            return (
                carry[0] | jnp.where(low == p, bit, 0),
                carry[1] | jnp.where(low == q, bit, 0),
            )

        marks.append(lax.fori_loop(0, list_ref.shape[0], mark, (jnp.int32(0), jnp.int32(0)), unroll=True))

    def listed(panel, part, index):
        return jnp.bitwise_and(jnp.right_shift(marks[panel][part], index), 1) > 0

    for wide in range(NP // 2):
        for part, v_ref in enumerate((vp_ref, vq_ref)):
            rows = pl.ds(part * order, order)
            cols = pl.ds(wide * WIDE, WIDE)
            loads[2 * wide + part].wait()
            raw = jnp.concatenate([v_ref[pl.ds(k * order, order), :] for k in (2 * wide, 2 * wide + 1)], axis=1)
            if wide:
                old = pl.ds(0, wide * WIDE)
                raw = raw - dot3((sh[rows, old], sl[rows, old]), (lh[cols, old], ll[cols, old]))
            solved = dot3(split(raw), (ih[wide], il[wide]))
            for a in range(RB):
                piece = jnp.where(listed(2 * wide // (NP // 2), part, a), solved[a * BS : (a + 1) * BS], 0.0)
                place = pl.ds(part * order + a * BS, BS)
                sh[place, cols], sl[place, cols] = split(piece)
                if part == 0:
                    for k in (2 * wide, 2 * wide + 1):
                        sf[k, pl.ds(a * BS, BS), :] = piece[:, (k % 2) * BS : (k % 2 + 1) * BS]

    loads[-1].wait()

    def update(u, carry):
        rows = pl.ds(0, order)
        cols = pl.ds(pl.multiple_of(order + u * WIDE, WIDE), WIDE)
        term = dot3((sh[rows, :], sl[rows, :]), (sh[cols, :], sl[cols, :]))
        for a in range(RB):
            for b in range(2):
                place = pl.ds(a * BS * RB + 2 * u + b, BS, RB)
                out_ref[place, :] = front_ref[place, :] - term[a * BS : (a + 1) * BS, b * BS : (b + 1) * BS]
        return carry

    lax.fori_loop(0, RB // 2, update, 0)

    for k in range(NP):
        slot = slots_ref[k]

        @pl.when(slot % GRID == q)
        def _():
            for a in range(RB):
                place = pl.ds(a * BS * RB + slot // GRID, BS, RB)
                number = jnp.int32(NP)
                for i in range(NP):
                    number = jnp.where(slots_ref[i] == a * GRID + p, i, number)

                @pl.when((number >= NP) & listed(k // (NP // 2), 0, a))
                def _():
                    out_ref[place, :] = sf[k, pl.ds(a * BS, BS), :]

                @pl.when((number < NP) & ((number >= NP // 2) | (k < NP // 2)))
                def _():
                    start = (FIRST[k] + jnp.maximum(number - k, 0)) * BS
                    piece = l_ref[pl.ds(pl.multiple_of(start, BS), BS), :]
                    out_ref[place, :] = jnp.where(number >= k, piece, 0.0)


def update(slots, first, second, front, vp, vq, lower, inverses):
    order = NP * BS
    return pl.pallas_call(
        update_kernel,
        out_shape=jax.ShapeDtypeStruct(front.shape, jnp.float32),
        in_specs=[SMEM] * 3 + [ANY] * 3 + [VMEM] * 2,
        out_specs=VMEM,
        scratch_shapes=[
            pltpu.VMEM(front.shape, jnp.float32),
            pltpu.VMEM(vp.shape, jnp.float32),
            pltpu.VMEM(vq.shape, jnp.float32),
            pltpu.VMEM((2 * RB * BS, order), jnp.bfloat16),
            pltpu.VMEM((2 * RB * BS, order), jnp.bfloat16),
            pltpu.VMEM((NP, RB * BS, BS), jnp.float32),
            pltpu.VMEM((order, order), jnp.bfloat16),
            pltpu.VMEM((order, order), jnp.bfloat16),
            pltpu.VMEM((NP // 2, WIDE, WIDE), jnp.bfloat16),
            pltpu.VMEM((NP // 2, WIDE, WIDE), jnp.bfloat16),
            pltpu.SemaphoreType.DMA((NP + 1,)),
        ],
        compiler_params=pltpu.CompilerParams(vmem_limit_bytes=60 * 2**20),
        name="update",
    )(slots, first, second, front, vp, vq, lower, inverses)


def on_device(front, block_slots, rows_first, rows_second):
    flat = front.reshape(RB * BS * RB, BS)
    vp, vq, lower, inverses = gather_and_factor(block_slots, flat)
    return update(block_slots, rows_first, rows_second, flat, vp, vq, lower, inverses).reshape(front.shape)


def solution(mesh):
    placed = (P(None, "row", None, None, "col", None), P(), P(), P())
    return jax.shard_map(
        on_device,
        mesh=mesh,
        in_specs=placed,
        out_specs=P(None, "row", None, None, "col", None),
        check_vma=False,
    )
```
